256 devices in a mesh: ctx: 64 (over z, y, core), ch: 4 (over x).
Axes of the slice: x: 4, y: 4, z: 8, core: 2. Of those that a mesh axis runs over, the one named last changes fastest.
Arguments:
- query_branch: bfloat16 [16384, 2048], P('ctx', 'ch'), may hold values from -6 to 6
- key_branch: bfloat16 [16384, 2048], P('ctx', 'ch'), may hold values from -6 to 6
- value_branch: bfloat16 [16384, 2048], P('ctx', 'ch'), may hold values from -6 to 6
- grad_output: bfloat16 [16384, 2048], P('ctx', 'ch'), may hold values from -6 to 6
- conv_output: bfloat16 [16384, 2048], P('ctx', 'ch'), may hold values from -6 to 6
- filters: float32 [16384, 512], P('ctx'), may hold values from -0.0625 to 0.0625
- genome_blocks: int32 [8], replicated, may hold values from 1 to 32, 64 in all
Outputs:
- grad_query: bfloat16 [16384, 2048], P('ctx', 'ch')
- grad_key: bfloat16 [16384, 2048], P('ctx', 'ch')
- grad_value: bfloat16 [16384, 2048], P('ctx', 'ch')
- grad_filters: float32 [16384, 512], P('ctx', 'ch')
The draws below stay inside these ranges and needn't reach their ends.
Inputs may be any that keep to these rules, and one draw needn't show every extreme that they name: `genome_blocks`: the genomes lie in order and fill the row; the longest covers exactly 32 shards.
All inputs are finite; a program needn't handle non-finite values.
Results may differ from the reference program's by a relative error of at most 0.001.
Values sent between devices are 32-bit elements; how exact they have to be, the bound alone decides.
No kernel may reach another device: no remote copies, remote signals or barrier semaphores. Data moves between devices by JAX's collectives and lax.ppermute only.
A program may use at most 128 MiB of HBM per device.

```python
import math
import jax
import jax.numpy as jnp
import numpy as np
from jax import lax

TOK_DEV = 256
CHANNELS = 2048
FILTERS = 512
TOKENS = 16384
MOST = 32
GENOMES = 8
N_CTX = 64


def block_scale(stream_key, extent, pieces, least, top_value):
    factor_of, own = 1.0, jax.random.fold_in(stream_key, 6)
    for dim, parts in pieces:
        draws = jnp.exp(jax.random.uniform(jax.random.fold_in(own, dim), (parts,), jnp.float32, least / len(pieces), top_value / len(pieces)))
        factor_of = factor_of * jnp.repeat(draws, extent[dim] // parts).reshape([-1 if axis == dim else 1 for axis in range(len(extent))])
    return factor_of


def profile(count, total, bound, skew):
    weights = [(1 << 20) // math.isqrt(grade ** skew) + 1 for grade in range(2, count + 1)]
    surplus, given = total - bound - (count - 1), [1] * (count - 1)
    while surplus > 0:
        free = [i for i in range(count - 1) if given[i] < bound]
        mass, left = sum([weights[i] for i in free]), surplus
        for i in free:
            more = min(bound - given[i], max(1, left * weights[i] // mass), surplus)
            given[i] = given[i] + more
            surplus = surplus - more
    return np.array([bound] + given)


def ragged(stream_key, number_of, total, bound, skew):
    if number_of == 2:
        one = jax.random.randint(stream_key, (), max(1, total - bound), min(bound, total - 1) + 1)
        return jnp.stack([one, total - one])
    tallies = jnp.asarray(profile(number_of, total, bound, skew), jnp.int32)
    twos = (number_of - 1) // 2
    giver, sink = tallies[1:1 + 2 * twos:2], tallies[2:2 + 2 * twos:2]
    slack = jnp.minimum(giver - 1, bound - sink)
    shifted = jax.random.randint(jax.random.fold_in(stream_key, 1), (twos,), 0, 1 << 20) % (slack + 1)
    tallies = tallies.at[1:1 + 2 * twos:2].set(giver - shifted).at[2:2 + 2 * twos:2].set(sink + shifted)
    return tallies[jax.random.permutation(jax.random.fold_in(stream_key, 2), number_of)]


def bell_draw(rng, extent, deviation, most, pieces=(), dtype=jnp.bfloat16):
    loudness = block_scale(rng, extent, pieces, -0.22, 0.18) if pieces else 1.0
    values = jax.random.normal(rng, extent, jnp.float32) * deviation * loudness
    return jnp.minimum(jnp.maximum(values, -most), most).astype(dtype)


def setup_inputs(seed: int = 0) -> dict:
    key_of = jax.random.split(jax.random.key(seed), 8)
    return {
        "query_branch": bell_draw(key_of[0], (TOKENS, CHANNELS), 1.0, 6.0, ((0, 64), (1, 4))),
        "key_branch": bell_draw(key_of[1], (TOKENS, CHANNELS), 1.0, 6.0, ((0, 64), (1, 4))),
        "value_branch": bell_draw(key_of[2], (TOKENS, CHANNELS), 1.0, 6.0, ((0, 64), (1, 4))),
        "grad_output": bell_draw(key_of[3], (TOKENS, CHANNELS), 1.0, 6.0, ((0, 64), (1, 4))),
        "conv_output": bell_draw(key_of[4], (TOKENS, CHANNELS), 1.0, 6.0, ((0, 64), (1, 4))),
        "filters": bell_draw(key_of[5], (TOKENS, FILTERS), (MOST * TOK_DEV) ** -0.5, 0.0625, ((0, 64),), jnp.float32),
        "genome_blocks": ragged(key_of[6], GENOMES, N_CTX, MOST, 2).astype(jnp.int32),
    }


def reference(query_branch, key_branch, value_branch, grad_output, conv_output, filters, genome_blocks):
    length, channels = query_branch.shape
    repeats = channels // filters.shape[1]
    query32 = query_branch.astype(jnp.float32)
    key32 = key_branch.astype(jnp.float32)
    gated = query32 * key32
    carried = grad_output.astype(jnp.float32) * value_branch.astype(jnp.float32)
    grad_value = (grad_output.astype(jnp.float32) * conv_output.astype(jnp.float32)).astype(jnp.bfloat16)
    ends = (jnp.cumsum(genome_blocks) * TOK_DEV).astype(jnp.int32)
    places = jnp.arange(length).astype(jnp.int32)
    owners = jnp.sum((ends[None, :] <= places[:, None]).astype(jnp.int32), axis=1)
    full_len = 2 * length
    filter_spec = jnp.tile(jnp.conj(jnp.fft.rfft(filters, n=full_len, axis=0)), (1, repeats))

    def one_genome(state, genome):
        back, lag_sum = state
        inside = (owners == genome).astype(jnp.float32)[:, None]
        carried_spec = jnp.fft.rfft(carried * inside, n=full_len, axis=0)
        gated_spec = jnp.fft.rfft(gated * inside, n=full_len, axis=0)
        back = back + jnp.fft.irfft(carried_spec * filter_spec, n=full_len, axis=0)[:length] * inside
        cross = jnp.fft.irfft(carried_spec * jnp.conj(gated_spec), n=full_len, axis=0)[:length]
        lag_sum = lag_sum + cross.reshape(length, repeats, -1).sum(axis=1)
        return (back, lag_sum), None

    start = (jnp.zeros((length, channels), jnp.float32), jnp.zeros(filters.shape, jnp.float32))
    (back, lag_sum), _ = lax.scan(one_genome, start, jnp.arange(GENOMES).astype(jnp.int32))
    grad_query = (back * key32).astype(jnp.bfloat16)
    grad_key = (back * query32).astype(jnp.bfloat16)
    grad_filters = lag_sum * (TOKENS ** -0.5)
    return grad_query, grad_key, grad_value, grad_filters
```

```python
import functools

import jax
import jax.numpy as jnp
import ml_dtypes
import numpy as np
from jax import lax
from jax.experimental import pallas as pl
from jax.experimental.pallas import tpu as pltpu
from jax.sharding import PartitionSpec as P

BLOCK = 256
LANES = 128
OWN = 8
PLANES = 4
NCTX = 64
MOST = 32
GENOMES = 8
UNROLL = 4
IN_ROWS = 36
OUT_ROWS = 20
F32 = jnp.float32
BF16 = jnp.bfloat16


def split_table(table):
    high = table.astype(ml_dtypes.bfloat16)
    low = (table - high.astype(np.float64)).astype(ml_dtypes.bfloat16)
    return high, low


def dft_tables():
    freq = np.arange(BLOCK)
    sample = np.arange(BLOCK)
    phase = (sample[:, None] * (2 * freq[None, :] + 1)) % (4 * BLOCK)
    angle = phase * (np.pi / (2 * BLOCK))
    forward = np.concatenate([np.cos(angle), -np.sin(angle)], axis=1)
    inverse = forward.T / BLOCK
    return split_table(forward) + split_table(inverse)


def dot3(x, high, low):
    x_high = x.astype(BF16)
    x_low = (x - x_high.astype(F32)).astype(BF16)
    total = jnp.dot(x_low, high, preferred_element_type=F32)
    total = total + jnp.dot(x_high, low, preferred_element_type=F32)
    return total + jnp.dot(x_high, high, preferred_element_type=F32)


def pack_kernel(q_ref, k_ref, v_ref, g_ref, f_ref, out_ref, turned):
    for which, (a_ref, b_ref) in enumerate(((q_ref, k_ref), (g_ref, v_ref))):
        product = a_ref[...].astype(F32) * b_ref[...].astype(F32)
        for half in range(2):
            turned[half] = product[half * LANES : (half + 1) * LANES, :].T
        for half in range(2):
            for quarter in range(PLANES):
                for r in range(2):
                    rows = turned[half, pl.ds(LANES * quarter + r, NCTX, stride=2), :]
                    first = 16 * which + 8 * half + 2 * quarter + r
                    out_ref[pl.ds(first, NCTX, stride=IN_ROWS), :] = rows
    for half in range(2):
        turned[half, 0:LANES, :] = f_ref[half * LANES : (half + 1) * LANES, :].T
        for r in range(2):
            rows = turned[half, pl.ds(r, NCTX, stride=2), :]
            out_ref[pl.ds(32 + 2 * half + r, NCTX, stride=IN_ROWS), :] = rows


def signs():
    lane = lax.broadcasted_iota(jnp.int32, (1, BLOCK), 1)
    return (1 - 2 * (lane % 2)).astype(F32)


def load4(ref, row):
    return [ref[pl.ds(row, OWN), pl.ds(LANES * i, LANES)] for i in range(4)]


def store4(ref, row, values):
    for i in range(4):
        ref[pl.ds(row, OWN), pl.ds(LANES * i, LANES)] = values[i]


def add_conj(total, first, second):
    out = list(total)
    for i in range(2):
        a_re, a_im, b_re, b_im = first[i], first[i + 2], second[i], second[i + 2]
        out[i] = out[i] + (a_re * b_re + a_im * b_im)
        out[i + 2] = out[i + 2] + (a_re * b_im - a_im * b_re)
    return tuple(out)


def sweep(first_ref, first_row, second_ref, second_row, count, start):
    def step(c, total):
        for u in range(UNROLL):
            a = load4(first_ref, pl.multiple_of(OWN * (first_row + UNROLL * c + u), OWN))
            b = load4(second_ref, pl.multiple_of(OWN * (second_row + UNROLL * c + u), OWN))
            total = add_conj(total, a, b)
        return total

    return lax.fori_loop(0, (count + UNROLL - 1) // UNROLL, step, start)


def lag_kernel(
    genome_ref, plane_ref, x_ref, fh_ref, fl_ref, ih_ref, il_ref,
    lag_ref, carried_ref, gated, lags, flat, place,
):
    def mark(g, begin):
        count = genome_ref[g]

        def one(b, _):
            place[begin + b] = begin + b + UNROLL * g
            return 0

        lax.fori_loop(0, count, one, 0)
        return begin + count

    lax.fori_loop(0, GENOMES, mark, jnp.int32(0))
    carried_ref[...] = jnp.zeros_like(carried_ref)
    lags[...] = jnp.zeros_like(lags)
    gated[OWN * NCTX :, :] = jnp.zeros((OWN * UNROLL, 2 * BLOCK), F32)
    group = 16
    for part in range(NCTX // group):
        for which in range(2):
            rows = []
            for s in range(part * group, (part + 1) * group):
                base = IN_ROWS * s + 16 * which
                rows.append(
                    jnp.concatenate([x_ref[base : base + 8, :], x_ref[base + 8 : base + 16, :]], 1)
                )
            spec = dot3(jnp.concatenate(rows, 0), fh_ref[...], fl_ref[...])
            if which == 0:
                gated[OWN * group * part : OWN * group * (part + 1), :] = spec
            else:
                for i in range(group):
                    row = pl.multiple_of(OWN * place[part * group + i], OWN)
                    carried_ref[pl.ds(row, OWN), :] = spec[OWN * i : OWN * (i + 1), :]

    def genome(g, begin):
        count = genome_ref[g]

        def one_lag(d, _):
            row = pl.multiple_of(OWN * d, OWN)
            start = tuple(load4(lags, row))
            store4(
                lags,
                row,
                sweep(gated, begin, carried_ref, begin + UNROLL * g + d, count - d, start),
            )
            return 0

        lax.fori_loop(0, count, one_lag, 0)
        return begin + count

    lax.fori_loop(0, GENOMES, genome, jnp.int32(0))
    sign = signs()
    here, after = lags[: OWN * MOST, :], lags[OWN : OWN * (MOST + 1), :]
    spec = jnp.concatenate(
        [here[:, :BLOCK] + sign * after[:, BLOCK:], here[:, BLOCK:] - sign * after[:, :BLOCK]], 1
    )
    rows = dot3(spec, ih_ref[...], il_ref[...])
    for half in range(2):
        flat[half] = rows[:, half * LANES : (half + 1) * LANES]
    for quarter in range(PLANES):
        slot = lax.rem(quarter + PLANES - plane_ref[0], PLANES)
        for half in range(2):
            for r in range(2):
                rows = flat[half, pl.ds(2 * quarter + r, MOST, stride=OWN), :]
                lag_ref[slot, pl.ds(2 * half + r, MOST, stride=4), :] = rows


def back_kernel(
    genome_ref, plane_ref, carried_ref, f0_ref, f1_ref, f2_ref, f3_ref,
    fh_ref, fl_ref, ih_ref, il_ref, out_ref, filt, back, flat,
):
    for k, f_ref in enumerate((f0_ref, f1_ref, f2_ref, f3_ref)):
        quarter = lax.rem(plane_ref[0] + PLANES - k, PLANES)
        for half in range(2):
            for r in range(2):
                rows = f_ref[pl.ds(2 * half + r, MOST, stride=4), :]
                flat[half, pl.ds(2 * quarter + r, MOST, stride=OWN), :] = rows
    spec = dot3(jnp.concatenate([flat[0], flat[1]], 1), fh_ref[...], fl_ref[...])
    sign = signs()
    prior = jnp.concatenate([jnp.zeros((OWN, 2 * BLOCK), F32), spec[: OWN * (MOST - 1), :]], 0)
    filt[: OWN * MOST, :] = spec + jnp.concatenate(
        [-sign * prior[:, BLOCK:], sign * prior[:, :BLOCK]], 1
    )
    filt[OWN * MOST :, :] = jnp.zeros((OWN * UNROLL, 2 * BLOCK), F32)
    nothing = (jnp.zeros((OWN, LANES), F32),) * 4

    def genome(g, begin):
        count = genome_ref[g]

        def one_block(b, _):
            row = pl.multiple_of(OWN * (begin + b), OWN)
            store4(
                back, row, sweep(filt, 0, carried_ref, begin + UNROLL * g + b, count - b, nothing)
            )
            return 0

        lax.fori_loop(0, count, one_block, 0)
        return begin + count

    lax.fori_loop(0, GENOMES, genome, jnp.int32(0))
    group = 16
    for part in range(NCTX // group):
        rows = dot3(
            back[OWN * group * part : OWN * group * (part + 1), :], ih_ref[...], il_ref[...]
        )
        for i in range(group):
            base = OUT_ROWS * (part * group + i)
            for half in range(2):
                out_ref[base + 8 * half : base + 8 * half + 8, :] = rows[
                    OWN * i : OWN * (i + 1), half * LANES : (half + 1) * LANES
                ]
    for i in range(NCTX):
        base = OUT_ROWS * i + 16
        out_ref[base : base + 4, :] = jnp.zeros((4, LANES), F32)


def unpack_kernel(scale, x_ref, q_ref, k_ref, gq_ref, gk_ref, gf_ref, turned):
    for half in range(2):
        for quarter in range(PLANES):
            for r in range(2):
                rows = x_ref[pl.ds(8 * half + 2 * quarter + r, NCTX, stride=OUT_ROWS), :]
                turned[half, pl.ds(LANES * quarter + r, NCTX, stride=2), :] = rows
        part = slice(half * LANES, (half + 1) * LANES)
        back = turned[half].T
        gq_ref[part, :] = (back * k_ref[part, :].astype(F32)).astype(BF16)
        gk_ref[part, :] = (back * q_ref[part, :].astype(F32)).astype(BF16)
    for half in range(2):
        for r in range(2):
            rows = x_ref[pl.ds(16 + 2 * half + r, NCTX, stride=OUT_ROWS), :]
            turned[half, pl.ds(r, NCTX, stride=2), :] = rows
        gf_ref[half * LANES : (half + 1) * LANES, :] = turned[half, 0:LANES, :].T * scale


VMEM = pl.BlockSpec(memory_space=pltpu.VMEM)
SMEM = pl.BlockSpec(memory_space=pltpu.SMEM)


def params():
    return pltpu.CompilerParams(vmem_limit_bytes=40 * 1024 * 1024)


def cost(flops, moved):
    return pl.CostEstimate(flops=flops, bytes_accessed=moved, transcendentals=0)


def shape(*dims):
    return jax.ShapeDtypeStruct(dims, F32)


def pack(q, k, v, g, f):
    return pl.pallas_call(
        pack_kernel,
        out_shape=shape(NCTX * IN_ROWS, LANES),
        in_specs=[VMEM] * 5,
        out_specs=VMEM,
        scratch_shapes=[pltpu.VMEM((2, 2 * BLOCK, LANES), F32)],
        compiler_params=params(),
        cost_estimate=cost(1 << 20, 3 << 20),
        name="pack",
    )(q, k, v, g, f)


def lag_part(genome_blocks, plane, x, tables):
    return pl.pallas_call(
        lag_kernel,
        out_shape=[
            shape(PLANES, 4 * MOST, LANES),
            shape(OWN * (NCTX + UNROLL * GENOMES), 2 * BLOCK),
        ],
        in_specs=[SMEM, SMEM] + [VMEM] * 5,
        out_specs=[VMEM, VMEM],
        scratch_shapes=[
            pltpu.VMEM((OWN * (NCTX + UNROLL), 2 * BLOCK), F32),
            pltpu.VMEM((OWN * (MOST + 1), 2 * BLOCK), F32),
            pltpu.VMEM((2, OWN * MOST, LANES), F32),
            pltpu.SMEM((NCTX,), jnp.int32),
        ],
        compiler_params=params(),
        cost_estimate=cost(4 << 30, 16 << 20),
        name="lag_part",
    )(genome_blocks, plane, x, *tables)


def back_part(genome_blocks, plane, carried, quarters, tables):
    return pl.pallas_call(
        back_kernel,
        out_shape=shape(NCTX * OUT_ROWS, LANES),
        in_specs=[SMEM, SMEM] + [VMEM] * 9,
        out_specs=VMEM,
        scratch_shapes=[
            pltpu.VMEM((OWN * (MOST + UNROLL), 2 * BLOCK), F32),
            pltpu.VMEM((OWN * NCTX, 2 * BLOCK), F32),
            pltpu.VMEM((2, OWN * MOST, LANES), F32),
        ],
        compiler_params=params(),
        cost_estimate=cost(4 << 30, 16 << 20),
        name="back_part",
    )(genome_blocks, plane, carried, *quarters, *tables)


def unpack(x, q, k, scale):
    half = jax.ShapeDtypeStruct(q.shape, BF16)
    return pl.pallas_call(
        functools.partial(unpack_kernel, scale),
        out_shape=[half, half, shape(BLOCK, LANES)],
        in_specs=[VMEM] * 3,
        out_specs=[VMEM] * 3,
        scratch_shapes=[pltpu.VMEM((2, 2 * BLOCK, LANES), F32)],
        compiler_params=params(),
        cost_estimate=cost(1 << 20, 3 << 20),
        name="unpack",
    )(x, q, k)


def shift(x, k):
    return lax.ppermute(x, "ch", [(i, (i + k) % PLANES) for i in range(PLANES)])


def exchange(x):
    return lax.all_to_all(x, "ctx", split_axis=0, concat_axis=0, tiled=True)


def local(q, k, v, g, c, filters, genome_blocks):
    tables = [jnp.asarray(t) for t in dft_tables()]
    plane = lax.axis_index("ch").astype(jnp.int32)
    plane_arr = plane.reshape(1)
    own_filters = lax.dynamic_slice_in_dim(filters, plane * LANES, LANES, 1)
    grad_value = (g.astype(F32) * c.astype(F32)).astype(BF16)
    sent = pack(q, k, v, g, own_filters).reshape(NCTX, IN_ROWS // 4, 4, LANES)
    got = exchange(sent)
    own_quarter = got[:MOST, 8].reshape(4 * MOST, LANES)
    quarters = [own_quarter] + [shift(own_quarter, i) for i in range(1, PLANES)]
    lag_slots, carried = lag_part(
        genome_blocks, plane_arr, got.reshape(NCTX * IN_ROWS, LANES), tables
    )
    lag_sum = lag_slots[0]
    for i in range(1, PLANES):
        lag_sum = lag_sum + shift(lag_slots[i], i)
    back = back_part(genome_blocks, plane_arr, carried, quarters, tables)
    back = back.reshape(NCTX, OUT_ROWS // 4, 4, LANES)
    back = lax.dynamic_update_slice(back, lag_sum.reshape(MOST, 1, 4, LANES), (0, 4, 0, 0))
    returned = exchange(back).reshape(NCTX * OUT_ROWS, LANES)
    scale = (NCTX * BLOCK) ** (-0.5)
    grad_query, grad_key, grad_filters = unpack(returned, q, k, scale)
    return grad_query, grad_key, grad_value, grad_filters


def solution(mesh):
    split = P("ctx", "ch")
    return jax.shard_map(
        local,
        mesh=mesh,
        in_specs=(split,) * 5 + (P("ctx", None), P()),
        out_specs=(split,) * 4,
        check_vma=False,
    )
```

```python
import functools

import jax
import jax.numpy as jnp
import ml_dtypes
import numpy as np
from jax import lax
from jax.experimental import pallas as pl
from jax.experimental.pallas import tpu as pltpu
from jax.sharding import PartitionSpec as P

BLOCK = 256
LANES = 128
OWN = 8
PLANES = 4
NCTX = 64
MOST = 32
GENOMES = 8
UNROLL = 4
GAP = UNROLL + 1
IN_ROWS = 36
OUT_ROWS = 20
F32 = jnp.float32
BF16 = jnp.bfloat16


def split_table(table):
    high = table.astype(ml_dtypes.bfloat16)
    low = (table - high.astype(np.float64)).astype(ml_dtypes.bfloat16)
    return np.concatenate([high, low, high], axis=0)


def dft_tables():
    freq = np.arange(BLOCK)
    sample = np.arange(BLOCK)
    phase = (sample[:, None] * (2 * freq[None, :] + 1)) % (4 * BLOCK)
    angle = phase * (np.pi / (2 * BLOCK))
    forward = np.concatenate([np.cos(angle), -np.sin(angle)], axis=1)
    return split_table(forward), split_table(forward.T / BLOCK)


def dot3(x, table):
    high = x.astype(BF16)
    low = (x - high.astype(F32)).astype(BF16)
    return jnp.dot(
        jnp.concatenate([low, high, high], 1), table[...], preferred_element_type=F32
    )


def pack_kernel(
    plane_ref, q_hbm, k_hbm, v_hbm, g_hbm, f_hbm, out_ref, q_ref, k_ref, v_ref, g_ref, f_ref,
    turned, sems,
):
    column = pl.multiple_of(plane_ref[0] * LANES, LANES)
    pairs = (
        (g_hbm, g_ref), (v_hbm, v_ref), (q_hbm, q_ref), (k_hbm, k_ref),
        (f_hbm.at[:, pl.ds(column, LANES)], f_ref),
    )
    copies = [pltpu.make_async_copy(a, b, sems.at[i]) for i, (a, b) in enumerate(pairs)]
    for copy in copies:
        copy.start()
    for which, (a_ref, b_ref, first_copy) in enumerate(((g_ref, v_ref, 0), (q_ref, k_ref, 2))):
        copies[first_copy].wait()
        copies[first_copy + 1].wait()
        product = a_ref[...].astype(F32) * b_ref[...].astype(F32)
        for half in range(2):
            turned[half] = product[half * LANES : (half + 1) * LANES, :].T
        for half in range(2):
            for quarter in range(PLANES):
                for r in range(2):
                    rows = turned[half, pl.ds(LANES * quarter + r, NCTX, stride=2), :]
                    first = 16 * (1 - which) + 8 * half + 2 * quarter + r
                    out_ref[pl.ds(first, NCTX, stride=IN_ROWS), :] = rows
    copies[4].wait()
    for half in range(2):
        turned[half, 0:LANES, :] = f_ref[half * LANES : (half + 1) * LANES, :].T
        for r in range(2):
            rows = turned[half, pl.ds(r, NCTX, stride=2), :]
            out_ref[pl.ds(32 + 2 * half + r, NCTX, stride=IN_ROWS), :] = rows


def signs():
    lane = lax.broadcasted_iota(jnp.int32, (1, BLOCK), 1)
    return (1 - 2 * (lane % 2)).astype(F32)


def load4(ref, row):
    return [ref[pl.ds(row, OWN), pl.ds(LANES * i, LANES)] for i in range(4)]


def store4(ref, row, values):
    for i in range(4):
        ref[pl.ds(row, OWN), pl.ds(LANES * i, LANES)] = values[i]


def add_conj(total, first, second):
    out = list(total)
    for i in range(2):
        a_re, a_im, b_re, b_im = first[i], first[i + 2], second[i], second[i + 2]
        out[i] = out[i] + (a_re * b_re + a_im * b_im)
        out[i + 2] = out[i + 2] + (a_re * b_im - a_im * b_re)
    return tuple(out)


def lag_kernel(
    genome_ref, plane_ref, x_ref, fwd_ref, inv_ref, lag_ref, carried_ref, gated, lags, flat, place,
):
    def mark(g, begin):
        count = genome_ref[g]

        def one(b, _):
            place[begin + b] = begin + b + GAP * g
            return 0

        lax.fori_loop(0, count, one, 0)
        row = pl.multiple_of(OWN * (begin + count + GAP * g), OWN)
        carried_ref[pl.ds(row, OWN * GAP), :] = jnp.zeros((OWN * GAP, 2 * BLOCK), F32)
        return begin + count

    lax.fori_loop(0, GENOMES, mark, jnp.int32(0))
    lags[...] = jnp.zeros_like(lags)
    gated[OWN * NCTX :, :] = jnp.zeros((OWN * UNROLL, 2 * BLOCK), F32)
    group = 32
    for part in range(NCTX // group):
        for which in range(2):
            rows = []
            for s in range(part * group, (part + 1) * group):
                base = IN_ROWS * s + 16 * which
                rows.append(
                    jnp.concatenate([x_ref[base : base + 8, :], x_ref[base + 8 : base + 16, :]], 1)
                )
            spec = dot3(jnp.concatenate(rows, 0), fwd_ref)
            if which == 0:
                gated[OWN * group * part : OWN * group * (part + 1), :] = spec
            else:
                for i in range(group):
                    row = pl.multiple_of(OWN * place[part * group + i], OWN)
                    carried_ref[pl.ds(row, OWN), :] = spec[OWN * i : OWN * (i + 1), :]

    def genome(g, begin):
        count = genome_ref[g]
        first = begin + GAP * g

        def two_lags(half, _):
            d = 2 * half

            def step(c, totals):
                low, high = totals
                s = UNROLL * c
                after = load4(carried_ref, pl.multiple_of(OWN * (first + d + s), OWN))
                for u in range(UNROLL):
                    a = load4(gated, pl.multiple_of(OWN * (begin + s + u), OWN))
                    low = add_conj(low, a, after)
                    after = load4(
                        carried_ref, pl.multiple_of(OWN * (first + d + s + u + 1), OWN)
                    )
                    high = add_conj(high, a, after)
                return low, high

            row = pl.multiple_of(OWN * d, OWN)
            start = (tuple(load4(lags, row)), tuple(load4(lags, row + OWN)))
            chunks = (count - d + UNROLL - 1) // UNROLL
            low, high = lax.fori_loop(0, chunks, step, start)
            store4(lags, row, low)
            store4(lags, row + OWN, high)
            return 0

        lax.fori_loop(0, (count + 1) // 2, two_lags, 0)
        return begin + count

    lax.fori_loop(0, GENOMES, genome, jnp.int32(0))
    sign = signs()
    here, after = lags[: OWN * MOST, :], lags[OWN : OWN * (MOST + 1), :]
    spec = jnp.concatenate(
        [here[:, :BLOCK] + sign * after[:, BLOCK:], here[:, BLOCK:] - sign * after[:, :BLOCK]], 1
    )
    rows = dot3(spec, inv_ref)
    for half in range(2):
        flat[half] = rows[:, half * LANES : (half + 1) * LANES]
    for quarter in range(PLANES):
        slot = lax.rem(quarter + PLANES - plane_ref[0], PLANES)
        for half in range(2):
            for r in range(2):
                rows = flat[half, pl.ds(2 * quarter + r, MOST, stride=OWN), :]
                lag_ref[slot, pl.ds(2 * half + r, MOST, stride=4), :] = rows


def back_kernel(
    genome_ref, plane_ref, carried_ref, f0_ref, f1_ref, f2_ref, f3_ref, fwd_ref, back, filt, flat,
):
    for k, f_ref in enumerate((f0_ref, f1_ref, f2_ref, f3_ref)):
        quarter = lax.rem(plane_ref[0] + PLANES - k, PLANES)
        for half in range(2):
            for r in range(2):
                rows = f_ref[pl.ds(2 * half + r, MOST, stride=4), :]
                flat[half, pl.ds(2 * quarter + r, MOST, stride=OWN), :] = rows
    spec = dot3(jnp.concatenate([flat[0], flat[1]], 1), fwd_ref)
    sign = signs()
    prior = jnp.concatenate([jnp.zeros((OWN, 2 * BLOCK), F32), spec[: OWN * (MOST - 1), :]], 0)
    filt[:OWN, :] = jnp.zeros((OWN, 2 * BLOCK), F32)
    filt[OWN : OWN * (MOST + 1), :] = spec + jnp.concatenate(
        [-sign * prior[:, BLOCK:], sign * prior[:, :BLOCK]], 1
    )
    filt[OWN * (MOST + 1) :, :] = jnp.zeros((OWN * UNROLL, 2 * BLOCK), F32)
    nothing = (jnp.zeros((OWN, LANES), F32),) * 4

    def genome(g, begin):
        count = genome_ref[g]
        first = begin + GAP * g

        def two_blocks(half, _):
            b = 2 * half

            def step(c, totals):
                low, high = totals
                t = UNROLL * c
                before = load4(filt, pl.multiple_of(OWN * t, OWN))
                for u in range(UNROLL):
                    later = load4(carried_ref, pl.multiple_of(OWN * (first + b + t + u), OWN))
                    high = add_conj(high, before, later)
                    before = load4(filt, pl.multiple_of(OWN * (t + u + 1), OWN))
                    low = add_conj(low, before, later)
                return low, high

            chunks = (count - b + UNROLL - 1) // UNROLL
            low, high = lax.fori_loop(0, chunks, step, (nothing, nothing))
            row = pl.multiple_of(OWN * (begin + b), OWN)
            store4(back, row, low)
            store4(back, row + OWN, high)
            return 0

        lax.fori_loop(0, (count + 1) // 2, two_blocks, 0)
        return begin + count

    lax.fori_loop(0, GENOMES, genome, jnp.int32(0))


def finish_kernel(back, l0_ref, l1_ref, l2_ref, l3_ref, inv_ref, out_ref):
    group = 32
    for part in range(NCTX // group):
        rows = dot3(back[OWN * group * part : OWN * group * (part + 1), :], inv_ref)
        for i in range(group):
            base = OUT_ROWS * (part * group + i)
            for half in range(2):
                out_ref[base + 8 * half : base + 8 * half + 8, :] = rows[
                    OWN * i : OWN * (i + 1), half * LANES : (half + 1) * LANES
                ]
    for i in range(MOST):
        part = slice(4 * i, 4 * i + 4)
        total = (l0_ref[part, :] + l1_ref[part, :]) + (l2_ref[part, :] + l3_ref[part, :])
        out_ref[OUT_ROWS * i + 16 : OUT_ROWS * i + 20, :] = total
    for i in range(MOST, NCTX):
        out_ref[OUT_ROWS * i + 16 : OUT_ROWS * i + 20, :] = jnp.zeros((4, LANES), F32)


def unpack_kernel(scale, x_ref, q_ref, k_ref, gq_ref, gk_ref, gf_ref, turned):
    for half in range(2):
        for quarter in range(PLANES):
            for r in range(2):
                rows = x_ref[pl.ds(8 * half + 2 * quarter + r, NCTX, stride=OUT_ROWS), :]
                turned[half, pl.ds(LANES * quarter + r, NCTX, stride=2), :] = rows
        part = slice(half * LANES, (half + 1) * LANES)
        back = turned[half].T
        gq_ref[part, :] = (back * k_ref[part, :].astype(F32)).astype(BF16)
        gk_ref[part, :] = (back * q_ref[part, :].astype(F32)).astype(BF16)
    for half in range(2):
        for r in range(2):
            rows = x_ref[pl.ds(16 + 2 * half + r, NCTX, stride=OUT_ROWS), :]
            turned[half, pl.ds(r, NCTX, stride=2), :] = rows
        gf_ref[half * LANES : (half + 1) * LANES, :] = turned[half, 0:LANES, :].T * scale


VMEM = pl.BlockSpec(memory_space=pltpu.VMEM)
SMEM = pl.BlockSpec(memory_space=pltpu.SMEM)
HBM = pl.BlockSpec(memory_space=pltpu.HBM)


def params(mib=40):
    return pltpu.CompilerParams(vmem_limit_bytes=mib * 1024 * 1024)


def cost(flops, moved):
    return pl.CostEstimate(flops=flops, bytes_accessed=moved, transcendentals=0)


def shape(*dims):
    return jax.ShapeDtypeStruct(dims, F32)


def pack(plane, q, k, v, g, f):
    half = pltpu.VMEM(q.shape, BF16)
    return pl.pallas_call(
        pack_kernel,
        out_shape=shape(NCTX * IN_ROWS, LANES),
        in_specs=[SMEM] + [HBM] * 5,
        out_specs=VMEM,
        scratch_shapes=[half] * 4
        + [
            pltpu.VMEM((BLOCK, LANES), F32),
            pltpu.VMEM((2, 2 * BLOCK, LANES), F32),
            pltpu.SemaphoreType.DMA((5,)),
        ],
        compiler_params=params(60),
        cost_estimate=cost(1 << 20, 3 << 20),
        name="pack",
    )(plane, q, k, v, g, f)


def lag_part(genome_blocks, plane, x, tables):
    return pl.pallas_call(
        lag_kernel,
        out_shape=[
            shape(PLANES, 4 * MOST, LANES),
            shape(OWN * (NCTX + GAP * GENOMES), 2 * BLOCK),
        ],
        in_specs=[SMEM, SMEM] + [VMEM] * 3,
        out_specs=[VMEM, VMEM],
        scratch_shapes=[
            pltpu.VMEM((OWN * (NCTX + UNROLL), 2 * BLOCK), F32),
            pltpu.VMEM((OWN * (MOST + 1), 2 * BLOCK), F32),
            pltpu.VMEM((2, OWN * MOST, LANES), F32),
            pltpu.SMEM((NCTX,), jnp.int32),
        ],
        compiler_params=params(),
        cost_estimate=cost(1 << 36, 16 << 20),
        name="lag_part",
    )(genome_blocks, plane, x, *tables)


def back_part(genome_blocks, plane, carried, quarters, table):
    return pl.pallas_call(
        back_kernel,
        out_shape=shape(OWN * (NCTX + 1), 2 * BLOCK),
        in_specs=[SMEM, SMEM] + [VMEM] * 6,
        out_specs=VMEM,
        scratch_shapes=[
            pltpu.VMEM((OWN * (MOST + 1 + UNROLL), 2 * BLOCK), F32),
            pltpu.VMEM((2, OWN * MOST, LANES), F32),
        ],
        compiler_params=params(),
        cost_estimate=cost(1 << 36, 16 << 20),
        name="back_part",
    )(genome_blocks, plane, carried, *quarters, table)


def finish(back, lags, table):
    return pl.pallas_call(
        finish_kernel,
        out_shape=shape(NCTX * OUT_ROWS, LANES),
        in_specs=[VMEM] * 6,
        out_specs=VMEM,
        compiler_params=params(),
        cost_estimate=cost(1 << 28, 4 << 20),
        name="finish",
    )(back, *lags, table)


def unpack(x, q, k, scale):
    half = jax.ShapeDtypeStruct(q.shape, BF16)
    return pl.pallas_call(
        functools.partial(unpack_kernel, scale),
        out_shape=[half, half, shape(BLOCK, LANES)],
        in_specs=[VMEM] * 3,
        out_specs=[VMEM] * 3,
        scratch_shapes=[pltpu.VMEM((2, 2 * BLOCK, LANES), F32)],
        compiler_params=params(),
        cost_estimate=cost(1 << 20, 3 << 20),
        name="unpack",
    )(x, q, k)


def shift(x, k):
    return lax.ppermute(x, "ch", [(i, (i + k) % PLANES) for i in range(PLANES)])


def exchange(x):
    return lax.all_to_all(x, "ctx", split_axis=0, concat_axis=0, tiled=True)


def local(q, k, v, g, c, filters, genome_blocks):
    forward, inverse = [jnp.asarray(t) for t in dft_tables()]
    plane = lax.axis_index("ch").astype(jnp.int32).reshape(1)
    grad_value = (g.astype(F32) * c.astype(F32)).astype(BF16)
    sent = pack(plane, q, k, v, g, filters).reshape(NCTX, IN_ROWS // 4, 4, LANES)
    got = exchange(sent)
    own_quarter = got[:MOST, 8].reshape(4 * MOST, LANES)
    quarters = [own_quarter] + [shift(own_quarter, i) for i in range(1, PLANES)]
    slots, carried = lag_part(
        genome_blocks, plane, got.reshape(NCTX * IN_ROWS, LANES), (forward, inverse)
    )
    lags = [slots[0]] + [shift(slots[i], i) for i in range(1, PLANES)]
    back = back_part(genome_blocks, plane, carried, quarters, forward)
    out = finish(back, lags, inverse).reshape(NCTX, OUT_ROWS // 4, 4, LANES)
    returned = exchange(out).reshape(NCTX * OUT_ROWS, LANES)
    scale = (NCTX * BLOCK) ** (-0.5)
    grad_query, grad_key, grad_filters = unpack(returned, q, k, scale)
    return grad_query, grad_key, grad_value, grad_filters


def solution(mesh):
    split = P("ctx", "ch")
    return jax.shard_map(
        local,
        mesh=mesh,
        in_specs=(split,) * 5 + (P("ctx", None), P()),
        out_specs=(split,) * 4,
        check_vma=False,
    )
```

```python
import functools

import jax
import jax.numpy as jnp
import ml_dtypes
import numpy as np
from jax import lax
from jax.experimental import pallas as pl
from jax.experimental.pallas import tpu as pltpu
from jax.sharding import PartitionSpec as P

BLOCK = 256
LANES = 128
OWN = 8
PLANES = 4
NCTX = 64
MOST = 32
GENOMES = 8
UNROLL = 4
TILE = 4
GAP = UNROLL + TILE - 2
WIDE = 3 * BLOCK
IN_ROWS = 36
OUT_ROWS = 20
F32 = jnp.float32
BF16 = jnp.bfloat16


def split_table(table):
    high = table.astype(ml_dtypes.bfloat16)
    low = (table - high.astype(np.float64)).astype(ml_dtypes.bfloat16)
    return np.concatenate([high, low, high], axis=0)


def dft_tables():
    freq = np.arange(BLOCK)
    sample = np.arange(BLOCK)
    phase = (sample[:, None] * (2 * freq[None, :] + 1)) % (4 * BLOCK)
    angle = phase * (np.pi / (2 * BLOCK))
    forward = np.concatenate([np.cos(angle), -np.sin(angle)], axis=1)
    return split_table(forward), split_table(forward.T / BLOCK)


def dot3(x, table):
    high = x.astype(BF16)
    low = (x - high.astype(F32)).astype(BF16)
    return jnp.dot(
        jnp.concatenate([low, high, high], 1), table[...], preferred_element_type=F32
    )


def pack_kernel(
    plane_ref, q_hbm, k_hbm, v_hbm, g_hbm, f_hbm, out_ref, q_ref, k_ref, v_ref, g_ref, f_ref,
    turned, sems,
):
    column = pl.multiple_of(plane_ref[0] * LANES, LANES)
    pairs = (
        (g_hbm, g_ref), (v_hbm, v_ref), (q_hbm, q_ref), (k_hbm, k_ref),
        (f_hbm.at[:, pl.ds(column, LANES)], f_ref),
    )
    copies = [pltpu.make_async_copy(a, b, sems.at[i]) for i, (a, b) in enumerate(pairs)]
    for copy in copies:
        copy.start()

    for which, (a_ref, b_ref, first_copy) in enumerate(((g_ref, v_ref, 0), (q_ref, k_ref, 2))):
        copies[first_copy].wait()
        copies[first_copy + 1].wait()
        product = a_ref[...].astype(F32) * b_ref[...].astype(F32)
        for half in range(2):
            turned[half] = product[half * LANES : (half + 1) * LANES, :].T
        for half in range(2):
            for quarter in range(PLANES):
                for r in range(2):
                    rows = turned[half, pl.ds(LANES * quarter + r, NCTX, stride=2), :]
                    first = 16 * (1 - which) + 8 * half + 2 * quarter + r
                    out_ref[pl.ds(first, NCTX, stride=IN_ROWS), :] = rows
    copies[4].wait()
    for half in range(2):
        turned[half, 0:LANES, :] = f_ref[half * LANES : (half + 1) * LANES, :].T
        for r in range(2):
            rows = turned[half, pl.ds(r, NCTX, stride=2), :]
            out_ref[pl.ds(32 + 2 * half + r, NCTX, stride=IN_ROWS), :] = rows


def signs():
    lane = lax.broadcasted_iota(jnp.int32, (1, BLOCK), 1)
    return (1 - 2 * (lane % 2)).astype(F32)


def add_pairs(totals, pairs, first, second):
    for half in range(2):
        loaded = {}

        def load(name, view, index):
            if (name, index) not in loaded:
                loaded[name, index] = [
                    view[index, :, pl.ds(BLOCK * i + LANES * half, LANES)] for i in range(3)
                ]
            return loaded[name, index]

        out = {}
        for j, index, other in pairs:
            a, b = load("first", first, index), load("second", second, other)
            for i in range(3):
                lanes = pl.ds(BLOCK * i + LANES * half, LANES)
                if (j, i) not in out:
                    out[j, i] = totals[j, :, lanes]
                out[j, i] = out[j, i] + a[i] * b[i]
        for (j, i), value in out.items():
            totals[j, :, pl.ds(BLOCK * i + LANES * half, LANES)] = value


def lag_kernel(
    genome_ref, plane_ref, x_ref, fwd_ref, inv_ref, g_ref, c_ref,
    lag_ref, carried_ref, value_hbm, gated, lags, flat, value_ref, sem,
):
    value_ref[...] = (g_ref[...].astype(F32) * c_ref[...].astype(F32)).astype(BF16)
    give = pltpu.make_async_copy(value_ref, value_hbm, sem)
    give.start()
    end = jnp.int32(0)
    for g in range(GENOMES):
        end = end + genome_ref[g]
        carried_ref[pl.ds(end + GAP * g, GAP)] = jnp.zeros((GAP, OWN, WIDE), F32)
    lags[...] = jnp.zeros_like(lags)
    gated[NCTX:] = jnp.zeros((UNROLL, OWN, WIDE), F32)
    places, own, end = [], jnp.int32(0), genome_ref[0]
    for s in range(NCTX):
        if s:
            own = own + (s >= end).astype(jnp.int32)
            end = jnp.where(s >= end, end + genome_ref[own], end)
        places.append(s + GAP * own)
    group = 32
    for part in range(NCTX // group):
        for which in range(2):
            rows = []
            for s in range(part * group, (part + 1) * group):
                base = IN_ROWS * s + 16 * which
                rows.append(
                    jnp.concatenate([x_ref[base : base + 8, :], x_ref[base + 8 : base + 16, :]], 1)
                )
            spec = dot3(jnp.concatenate(rows, 0), fwd_ref).reshape(group, OWN, 2 * BLOCK)
            re, im = spec[:, :, :BLOCK], spec[:, :, BLOCK:]
            if which == 0:
                blocks = pl.ds(group * part, group)
                gated[blocks, :, 0:BLOCK] = re - im
                gated[blocks, :, BLOCK : 2 * BLOCK] = re
                gated[blocks, :, 2 * BLOCK : WIDE] = im
            else:
                less, more = im - re, re + im
                for i in range(group):
                    block = places[part * group + i]
                    carried_ref[block, :, 0:BLOCK] = re[i]
                    carried_ref[block, :, BLOCK : 2 * BLOCK] = less[i]
                    carried_ref[block, :, 2 * BLOCK : WIDE] = more[i]
    pairs = [(j, u, u + j) for u in range(UNROLL) for j in range(TILE)]

    def genome(g, begin):
        count = genome_ref[g]
        first = begin + GAP * g

        def tile(i, _):
            d = TILE * i

            totals = lags.at[pl.ds(d, TILE)]

            def step(c, _):
                s = UNROLL * c
                here = gated.at[pl.ds(begin + s, UNROLL)]
                after = carried_ref.at[pl.ds(first + d + s, UNROLL + TILE - 1)]
                add_pairs(totals, pairs, here, after)
                return 0

            lax.fori_loop(0, (count - d + UNROLL - 1) // UNROLL, step, 0)
            return 0

        lax.fori_loop(0, (count + TILE - 1) // TILE, tile, 0)
        return begin + count

    lax.fori_loop(0, GENOMES, genome, jnp.int32(0))
    sign = signs()
    k1, k2, k3 = [
        lags[: MOST + 1, :, BLOCK * i : BLOCK * (i + 1)].reshape(OWN * (MOST + 1), BLOCK)
        for i in range(3)
    ]
    re, im = k1 + k3, k1 + k2
    spec = jnp.concatenate(
        [re[: OWN * MOST] + sign * im[OWN:], im[: OWN * MOST] - sign * re[OWN:]], 1
    )
    rows = dot3(spec, inv_ref)
    for half in range(2):
        flat[half] = rows[:, half * LANES : (half + 1) * LANES]
    for quarter in range(PLANES):
        slot = lax.bitwise_xor(jnp.int32(quarter), plane_ref[0])
        for half in range(2):
            for r in range(2):
                rows = flat[half, pl.ds(2 * quarter + r, MOST, stride=OWN), :]
                lag_ref[slot, pl.ds(2 * half + r, MOST, stride=4), :] = rows
    give.wait()


def back_kernel(
    genome_ref, plane_ref, carried_ref, f0_ref, f1_ref, f2_ref, f3_ref, fwd_ref, back, filt, flat,
):
    for k, f_ref in enumerate((f0_ref, f1_ref, f2_ref, f3_ref)):
        quarter = lax.bitwise_xor(jnp.int32(k), plane_ref[0])
        for half in range(2):
            for r in range(2):
                rows = f_ref[pl.ds(2 * half + r, MOST, stride=4), :]
                flat[half, pl.ds(2 * quarter + r, MOST, stride=OWN), :] = rows
    spec = dot3(jnp.concatenate([flat[0], flat[1]], 1), fwd_ref)
    sign = signs()
    prior = jnp.concatenate([jnp.zeros((OWN, 2 * BLOCK), F32), spec[: OWN * (MOST - 1), :]], 0)
    re = spec[:, :BLOCK] - sign * prior[:, BLOCK:]
    im = spec[:, BLOCK:] + sign * prior[:, :BLOCK]
    head = TILE - 1
    filt[:head] = jnp.zeros((head, OWN, WIDE), F32)
    for i, value in enumerate((re - im, re, im)):
        filt[head : head + MOST, :, BLOCK * i : BLOCK * (i + 1)] = value.reshape(MOST, OWN, BLOCK)
    filt[head + MOST :] = jnp.zeros((UNROLL, OWN, WIDE), F32)
    pairs = [(j, u - j + head, u) for u in range(UNROLL) for j in range(TILE)]

    def genome(g, begin):
        count = genome_ref[g]
        first = begin + GAP * g

        def tile(i, _):
            b = TILE * i

            totals = back.at[pl.ds(begin + b, TILE)]
            totals[...] = jnp.zeros((TILE, OWN, WIDE), F32)

            def step(c, _):
                t = UNROLL * c
                taps = filt.at[pl.ds(t, UNROLL + TILE - 1)]
                later = carried_ref.at[pl.ds(first + b + t, UNROLL)]
                add_pairs(totals, pairs, taps, later)
                return 0

            lax.fori_loop(0, (count - b + UNROLL - 1) // UNROLL, step, 0)
            return 0

        lax.fori_loop(0, (count + TILE - 1) // TILE, tile, 0)
        return begin + count

    lax.fori_loop(0, GENOMES, genome, jnp.int32(0))


def finish_kernel(back, l0_ref, l1_ref, l2_ref, l3_ref, inv_ref, out_ref):
    group = 32
    for part in range(NCTX // group):
        k1, k2, k3 = [
            back[group * part : group * (part + 1), :, BLOCK * i : BLOCK * (i + 1)].reshape(
                OWN * group, BLOCK
            )
            for i in range(3)
        ]
        rows = dot3(jnp.concatenate([k1 + k3, k1 + k2], 1), inv_ref)
        for i in range(group):
            base = OUT_ROWS * (part * group + i)
            for half in range(2):
                out_ref[base + 8 * half : base + 8 * half + 8, :] = rows[
                    OWN * i : OWN * (i + 1), half * LANES : (half + 1) * LANES
                ]
    for i in range(MOST):
        part = slice(4 * i, 4 * i + 4)
        total = (l0_ref[part, :] + l1_ref[part, :]) + (l2_ref[part, :] + l3_ref[part, :])
        out_ref[OUT_ROWS * i + 16 : OUT_ROWS * i + 20, :] = total
    for i in range(MOST, NCTX):
        out_ref[OUT_ROWS * i + 16 : OUT_ROWS * i + 20, :] = jnp.zeros((4, LANES), F32)


def unpack_kernel(
    scale, x_ref, q_ref, k_ref, gq_hbm, gk_hbm, gf_hbm, gq_ref, gk_ref, gf_ref, turned, sems
):
    copies = []

    def send(source, target, rows):
        copy = pltpu.make_async_copy(source.at[rows], target.at[rows], sems.at[len(copies)])
        copy.start()
        copies.append(copy)

    for half in range(2):
        for quarter in range(PLANES):
            for r in range(2):
                rows = x_ref[pl.ds(8 * half + 2 * quarter + r, NCTX, stride=OUT_ROWS), :]
                turned[half, pl.ds(LANES * quarter + r, NCTX, stride=2), :] = rows
        part = pl.ds(half * LANES, LANES)
        back = turned[half].T
        gq_ref[part, :] = (back * k_ref[part, :].astype(F32)).astype(BF16)
        send(gq_ref, gq_hbm, part)
        gk_ref[part, :] = (back * q_ref[part, :].astype(F32)).astype(BF16)
        send(gk_ref, gk_hbm, part)
        for r in range(2):
            rows = x_ref[pl.ds(16 + 2 * half + r, NCTX, stride=OUT_ROWS), :]
            turned[half, pl.ds(r, NCTX, stride=2), :] = rows
        gf_ref[part, :] = turned[half, 0:LANES, :].T * scale
        send(gf_ref, gf_hbm, part)
    for copy in copies:
        copy.wait()


VMEM = pl.BlockSpec(memory_space=pltpu.VMEM)
SMEM = pl.BlockSpec(memory_space=pltpu.SMEM)
HBM = pl.BlockSpec(memory_space=pltpu.HBM)


def params(mib=40):
    return pltpu.CompilerParams(vmem_limit_bytes=mib * 1024 * 1024)


def cost(flops, moved):
    return pl.CostEstimate(flops=flops, bytes_accessed=moved, transcendentals=0)


def shape(*dims):
    return jax.ShapeDtypeStruct(dims, F32)


def in_hbm(*arrays):
    return [pltpu.with_memory_space_constraint(a, pltpu.HBM) for a in arrays]


def pack(plane, q, k, v, g, f):
    half = pltpu.VMEM(q.shape, BF16)
    return pl.pallas_call(
        pack_kernel,
        out_shape=pltpu.VMEM((NCTX * IN_ROWS, LANES), F32),
        in_specs=[SMEM] + [HBM] * 5,
        out_specs=VMEM,
        scratch_shapes=[half] * 4
        + [
            pltpu.VMEM((BLOCK, LANES), F32),
            pltpu.VMEM((2, 2 * BLOCK, LANES), F32),
            pltpu.SemaphoreType.DMA((5,)),
        ],
        compiler_params=params(),
        cost_estimate=cost(1 << 20, 3 << 20),
        name="pack",
    )(plane, *in_hbm(q, k, v, g, f))


def lag_part(genome_blocks, plane, x, tables, g, c):
    return pl.pallas_call(
        lag_kernel,
        out_shape=[
            shape(PLANES, 4 * MOST, LANES),
            shape(NCTX + GAP * GENOMES, OWN, WIDE),
            pltpu.HBM(g.shape, BF16),
        ],
        in_specs=[SMEM] * 2 + [VMEM] * 5,
        out_specs=[VMEM, VMEM, HBM],
        scratch_shapes=[
            pltpu.VMEM((NCTX + UNROLL, OWN, WIDE), F32),
            pltpu.VMEM((MOST + TILE, OWN, WIDE), F32),
            pltpu.VMEM((2, OWN * MOST, LANES), F32),
            pltpu.VMEM(g.shape, BF16),
            pltpu.SemaphoreType.DMA(()),
        ],
        compiler_params=params(),
        cost_estimate=cost(1 << 36, 16 << 20),
        name="lag_part",
    )(genome_blocks, plane, x, *tables, g, c)


def back_part(genome_blocks, plane, carried, quarters, table):
    return pl.pallas_call(
        back_kernel,
        out_shape=shape(NCTX + TILE, OWN, WIDE),
        in_specs=[SMEM, SMEM] + [VMEM] * 6,
        out_specs=VMEM,
        scratch_shapes=[
            pltpu.VMEM((TILE - 1 + MOST + UNROLL, OWN, WIDE), F32),
            pltpu.VMEM((2, OWN * MOST, LANES), F32),
        ],
        compiler_params=params(),
        cost_estimate=cost(1 << 36, 16 << 20),
        name="back_part",
    )(genome_blocks, plane, carried, *quarters, table)


def finish(back, lags, table):
    return pl.pallas_call(
        finish_kernel,
        out_shape=pltpu.VMEM((NCTX * OUT_ROWS, LANES), F32),
        in_specs=[VMEM] * 6,
        out_specs=VMEM,
        compiler_params=params(),
        cost_estimate=cost(1 << 28, 4 << 20),
        name="finish",
    )(back, *lags, table)


def unpack(x, q, k, scale):
    half = pltpu.VMEM(q.shape, BF16)
    wide = pltpu.VMEM((BLOCK, LANES), F32)
    return pl.pallas_call(
        functools.partial(unpack_kernel, scale),
        out_shape=[pltpu.HBM(a.shape, a.dtype) for a in (half, half, wide)],
        in_specs=[VMEM] * 3,
        out_specs=[HBM] * 3,
        scratch_shapes=[
            half,
            half,
            wide,
            pltpu.VMEM((2, 2 * BLOCK, LANES), F32),
            pltpu.SemaphoreType.DMA((6,)),
        ],
        compiler_params=params(),
        cost_estimate=cost(1 << 20, 3 << 20),
        name="unpack",
    )(x, q, k)


def shift(x, k):
    return lax.ppermute(x, "ch", [(i, i ^ k) for i in range(PLANES)])


def exchange(x):
    return lax.all_to_all(x, "ctx", split_axis=0, concat_axis=0, tiled=True)


def local(q, k, v, g, c, filters, genome_blocks):
    forward, inverse = [jnp.asarray(t) for t in dft_tables()]
    plane = lax.axis_index("ch").astype(jnp.int32).reshape(1)
    sent = pack(plane, q, k, v, g, filters)
    got = exchange(sent.reshape(NCTX, IN_ROWS // 4, 4, LANES))
    own_quarter = got[:MOST, 8].reshape(4 * MOST, LANES)
    quarters = [own_quarter] + [shift(own_quarter, i) for i in range(1, PLANES)]
    slots, carried, grad_value = lag_part(
        genome_blocks, plane, got.reshape(NCTX * IN_ROWS, LANES), (forward, inverse), g, c
    )
    lags = [slots[0]] + [shift(slots[i], i) for i in range(1, PLANES)]
    back = back_part(genome_blocks, plane, carried, quarters, forward)
    out = finish(back, lags, inverse).reshape(NCTX, OUT_ROWS // 4, 4, LANES)
    returned = exchange(out).reshape(NCTX * OUT_ROWS, LANES)
    scale = (NCTX * BLOCK) ** (-0.5)
    grad_query, grad_key, grad_filters = unpack(returned, q, k, scale)
    return grad_query, grad_key, grad_value, grad_filters


def solution(mesh):
    split = P("ctx", "ch")
    return jax.shard_map(
        local,
        mesh=mesh,
        in_specs=(split,) * 5 + (P("ctx", None), P()),
        out_specs=(split,) * 4,
        check_vma=False,
    )
```

```python
import functools

import jax
import jax.numpy as jnp
import ml_dtypes
import numpy as np
from jax import lax
from jax.experimental import pallas as pl
from jax.experimental.pallas import tpu as pltpu
from jax.sharding import PartitionSpec as P

BLOCK = 256
LANES = 128
OWN = 8
PLANES = 4
NCTX = 64
MOST = 32
GENOMES = 8
UNROLL = 4
TILE = 4
GAP = UNROLL + TILE - 2
WIDE = 3 * BLOCK
IN_ROWS = 36
OUT_ROWS = 20
F32 = jnp.float32
BF16 = jnp.bfloat16


def split_table(table):
    high = table.astype(ml_dtypes.bfloat16)
    low = (table - high.astype(np.float64)).astype(ml_dtypes.bfloat16)
    return np.concatenate([high, low, high], axis=0)


def dft_tables():
    freq = np.arange(BLOCK)
    sample = np.arange(BLOCK)
    phase = (sample[:, None] * (2 * freq[None, :] + 1)) % (4 * BLOCK)
    angle = phase * (np.pi / (2 * BLOCK))
    forward = np.concatenate([np.cos(angle), -np.sin(angle)], axis=1)
    return split_table(forward), split_table(forward.T / BLOCK)


def dot3(x, table):
    high = x.astype(BF16)
    low = (x - high.astype(F32)).astype(BF16)
    left = jnp.concatenate([low, high, high], 1)
    parts = [
        jnp.dot(left, table[:, i : i + BLOCK], preferred_element_type=F32)
        for i in range(0, table.shape[1], BLOCK)
    ]
    return jnp.concatenate(parts, 1) if len(parts) > 1 else parts[0]


def pack_kernel(
    plane_ref, q_hbm, k_hbm, v_hbm, g_hbm, f_hbm, out_ref, q_ref, k_ref, v_ref, g_ref, f_ref,
    turned, sems,
):
    column = pl.multiple_of(plane_ref[0] * LANES, LANES)
    pairs = (
        (g_hbm, g_ref), (v_hbm, v_ref), (q_hbm, q_ref), (k_hbm, k_ref),
        (f_hbm.at[:, pl.ds(column, LANES)], f_ref),
    )
    copies = [pltpu.make_async_copy(a, b, sems.at[i]) for i, (a, b) in enumerate(pairs)]
    for copy in copies[4:] + copies[:4]:
        copy.start()

    copies[4].wait()
    for half in range(2):
        turned[half, 0:LANES, :] = f_ref[half * LANES : (half + 1) * LANES, :].T
        for r in range(2):
            rows = turned[half, pl.ds(r, NCTX, stride=2), :]
            out_ref[pl.ds(32 + 2 * half + r, NCTX, stride=IN_ROWS), :] = rows
    for which, (a_ref, b_ref, first_copy) in enumerate(((g_ref, v_ref, 0), (q_ref, k_ref, 2))):
        copies[first_copy].wait()
        copies[first_copy + 1].wait()
        product = a_ref[...].astype(F32) * b_ref[...].astype(F32)
        for half in range(2):
            turned[half] = product[half * LANES : (half + 1) * LANES, :].T
        for half in range(2):
            for quarter in range(PLANES):
                for r in range(2):
                    rows = turned[half, pl.ds(LANES * quarter + r, NCTX, stride=2), :]
                    first = 16 * (1 - which) + 8 * half + 2 * quarter + r
                    out_ref[pl.ds(first, NCTX, stride=IN_ROWS), :] = rows


def signs():
    lane = lax.broadcasted_iota(jnp.int32, (1, BLOCK), 1)
    return (1 - 2 * (lane % 2)).astype(F32)


def add_pairs(totals, pairs, first, second):
    for half in range(2):
        loaded = {}

        def load(name, view, index):
            if (name, index) not in loaded:
                loaded[name, index] = [
                    view[index, :, pl.ds(BLOCK * i + LANES * half, LANES)] for i in range(3)
                ]
            return loaded[name, index]

        out = {}
        for j, index, other in pairs:
            a, b = load("first", first, index), load("second", second, other)
            for i in range(3):
                lanes = pl.ds(BLOCK * i + LANES * half, LANES)
                if (j, i) not in out:
                    out[j, i] = totals[j, :, lanes]
                out[j, i] = out[j, i] + a[i] * b[i]
        for (j, i), value in out.items():
            totals[j, :, pl.ds(BLOCK * i + LANES * half, LANES)] = value


def lag_kernel(
    genome_ref, plane_ref, x_ref, fwd_ref, inv_ref, g_ref, c_ref,
    lag_ref, carried_ref, value_hbm, gated, lags, flat, value_ref, sem,
):
    value_ref[...] = (g_ref[...].astype(F32) * c_ref[...].astype(F32)).astype(BF16)
    give = pltpu.make_async_copy(value_ref, value_hbm, sem)
    give.start()
    end = jnp.int32(0)
    for g in range(GENOMES):
        end = end + genome_ref[g]
        carried_ref[pl.ds(end + GAP * g, GAP)] = jnp.zeros((GAP, OWN, WIDE), F32)
    lags[...] = jnp.zeros_like(lags)
    gated[NCTX:] = jnp.zeros((UNROLL, OWN, WIDE), F32)
    places, own, end = [], jnp.int32(0), genome_ref[0]
    for s in range(NCTX):
        if s:
            own = own + (s >= end).astype(jnp.int32)
            end = jnp.where(s >= end, end + genome_ref[own], end)
        places.append(s + GAP * own)
    group = 32
    for part in range(NCTX // group):
        for which in range(2):
            rows = []
            for s in range(part * group, (part + 1) * group):
                base = IN_ROWS * s + 16 * which
                rows.append(
                    jnp.concatenate([x_ref[base : base + 8, :], x_ref[base + 8 : base + 16, :]], 1)
                )
            spec = dot3(jnp.concatenate(rows, 0), fwd_ref).reshape(group, OWN, 2 * BLOCK)
            re, im = spec[:, :, :BLOCK], spec[:, :, BLOCK:]
            if which == 0:
                blocks = pl.ds(group * part, group)
                gated[blocks, :, 0:BLOCK] = re - im
                gated[blocks, :, BLOCK : 2 * BLOCK] = re
                gated[blocks, :, 2 * BLOCK : WIDE] = im
            else:
                less, more = im - re, re + im
                for i in range(group):
                    block = places[part * group + i]
                    carried_ref[block, :, 0:BLOCK] = re[i]
                    carried_ref[block, :, BLOCK : 2 * BLOCK] = less[i]
                    carried_ref[block, :, 2 * BLOCK : WIDE] = more[i]
    pairs = [(j, u, u + j) for u in range(UNROLL) for j in range(TILE)]

    def genome(g, begin):
        count = genome_ref[g]
        first = begin + GAP * g

        def tile(i, _):
            d = TILE * i

            totals = lags.at[pl.ds(d, TILE)]

            def step(c, _):
                s = UNROLL * c
                here = gated.at[pl.ds(begin + s, UNROLL)]
                after = carried_ref.at[pl.ds(first + d + s, UNROLL + TILE - 1)]
                add_pairs(totals, pairs, here, after)
                return 0

            lax.fori_loop(0, (count - d + UNROLL - 1) // UNROLL, step, 0)
            return 0

        lax.fori_loop(0, (count + TILE - 1) // TILE, tile, 0)
        return begin + count

    lax.fori_loop(0, GENOMES, genome, jnp.int32(0))
    sign = signs()
    k1, k2, k3 = [
        lags[: MOST + 1, :, BLOCK * i : BLOCK * (i + 1)].reshape(OWN * (MOST + 1), BLOCK)
        for i in range(3)
    ]
    re, im = k1 + k3, k1 + k2
    spec = jnp.concatenate(
        [re[: OWN * MOST] + sign * im[OWN:], im[: OWN * MOST] - sign * re[OWN:]], 1
    )
    for part in range(2):
        top = OWN * MOST // 2 * part
        rows = dot3(spec[top : top + OWN * MOST // 2, :], inv_ref)
        for half in range(2):
            flat[half, top : top + OWN * MOST // 2, :] = rows[
                :, half * LANES : (half + 1) * LANES
            ]
    for quarter in range(PLANES):
        slot = lax.bitwise_xor(jnp.int32(quarter), plane_ref[0])
        for half in range(2):
            for r in range(2):
                rows = flat[half, pl.ds(2 * quarter + r, MOST, stride=OWN), :]
                lag_ref[slot, pl.ds(2 * half + r, MOST, stride=4), :] = rows
    give.wait()


def back_kernel(
    genome_ref, plane_ref, carried_ref, f0_ref, f1_ref, f2_ref, f3_ref, fwd_ref, back, filt, flat,
):
    for k, f_ref in enumerate((f0_ref, f1_ref, f2_ref, f3_ref)):
        quarter = lax.bitwise_xor(jnp.int32(k), plane_ref[0])
        for half in range(2):
            for r in range(2):
                rows = f_ref[pl.ds(2 * half + r, MOST, stride=4), :]
                flat[half, pl.ds(2 * quarter + r, MOST, stride=OWN), :] = rows
    spec = dot3(jnp.concatenate([flat[0], flat[1]], 1), fwd_ref)
    sign = signs()
    prior = jnp.concatenate([jnp.zeros((OWN, 2 * BLOCK), F32), spec[: OWN * (MOST - 1), :]], 0)
    re = spec[:, :BLOCK] - sign * prior[:, BLOCK:]
    im = spec[:, BLOCK:] + sign * prior[:, :BLOCK]
    head = TILE - 1
    filt[:head] = jnp.zeros((head, OWN, WIDE), F32)
    for i, value in enumerate((re - im, re, im)):
        filt[head : head + MOST, :, BLOCK * i : BLOCK * (i + 1)] = value.reshape(MOST, OWN, BLOCK)
    filt[head + MOST :] = jnp.zeros((UNROLL, OWN, WIDE), F32)
    pairs = [(j, u - j + head, u) for u in range(UNROLL) for j in range(TILE)]

    def genome(g, begin):
        count = genome_ref[g]
        first = begin + GAP * g

        def tile(i, _):
            b = TILE * i

            totals = back.at[pl.ds(begin + b, TILE)]
            totals[...] = jnp.zeros((TILE, OWN, WIDE), F32)

            def step(c, _):
                t = UNROLL * c
                taps = filt.at[pl.ds(t, UNROLL + TILE - 1)]
                later = carried_ref.at[pl.ds(first + b + t, UNROLL)]
                add_pairs(totals, pairs, taps, later)
                return 0

            lax.fori_loop(0, (count - b + UNROLL - 1) // UNROLL, step, 0)
            return 0

        lax.fori_loop(0, (count + TILE - 1) // TILE, tile, 0)
        return begin + count

    lax.fori_loop(0, GENOMES, genome, jnp.int32(0))


def finish_kernel(back, l0_ref, l1_ref, l2_ref, l3_ref, inv_ref, out_ref):
    group = 32
    for part in range(NCTX // group):
        k1, k2, k3 = [
            back[group * part : group * (part + 1), :, BLOCK * i : BLOCK * (i + 1)].reshape(
                OWN * group, BLOCK
            )
            for i in range(3)
        ]
        rows = dot3(jnp.concatenate([k1 + k3, k1 + k2], 1), inv_ref)
        for i in range(group):
            base = OUT_ROWS * (part * group + i)
            for half in range(2):
                out_ref[base + 8 * half : base + 8 * half + 8, :] = rows[
                    OWN * i : OWN * (i + 1), half * LANES : (half + 1) * LANES
                ]
    for i in range(MOST):
        part = slice(4 * i, 4 * i + 4)
        total = (l0_ref[part, :] + l1_ref[part, :]) + (l2_ref[part, :] + l3_ref[part, :])
        out_ref[OUT_ROWS * i + 16 : OUT_ROWS * i + 20, :] = total
    for i in range(MOST, NCTX):
        out_ref[OUT_ROWS * i + 16 : OUT_ROWS * i + 20, :] = jnp.zeros((4, LANES), F32)


def unpack_kernel(
    scale, x_ref, q_ref, k_ref, gq_hbm, gk_hbm, gf_hbm, gq_ref, gk_ref, gf_ref, turned, sems
):
    copies = []

    def send(source, target, rows):
        copy = pltpu.make_async_copy(source.at[rows], target.at[rows], sems.at[len(copies)])
        copy.start()
        copies.append(copy)

    for half in range(2):
        for quarter in range(PLANES):
            for r in range(2):
                rows = x_ref[pl.ds(8 * half + 2 * quarter + r, NCTX, stride=OUT_ROWS), :]
                turned[half, pl.ds(LANES * quarter + r, NCTX, stride=2), :] = rows
        part = pl.ds(half * LANES, LANES)
        back = turned[half].T
        gq_ref[part, :] = (back * k_ref[part, :].astype(F32)).astype(BF16)
        send(gq_ref, gq_hbm, part)
        gk_ref[part, :] = (back * q_ref[part, :].astype(F32)).astype(BF16)
        send(gk_ref, gk_hbm, part)
        for r in range(2):
            rows = x_ref[pl.ds(16 + 2 * half + r, NCTX, stride=OUT_ROWS), :]
            turned[half, pl.ds(r, NCTX, stride=2), :] = rows
        gf_ref[part, :] = turned[half, 0:LANES, :].T * scale
        send(gf_ref, gf_hbm, part)
    for copy in copies:
        copy.wait()


VMEM = pl.BlockSpec(memory_space=pltpu.VMEM)
SMEM = pl.BlockSpec(memory_space=pltpu.SMEM)
HBM = pl.BlockSpec(memory_space=pltpu.HBM)


def params(mib=40):
    return pltpu.CompilerParams(vmem_limit_bytes=mib * 1024 * 1024)


def cost(flops, moved):
    return pl.CostEstimate(flops=flops, bytes_accessed=moved, transcendentals=0)


def shape(*dims):
    return jax.ShapeDtypeStruct(dims, F32)


def in_hbm(*arrays):
    return [pltpu.with_memory_space_constraint(a, pltpu.HBM) for a in arrays]


def pack(plane, q, k, v, g, f):
    half = pltpu.VMEM(q.shape, BF16)
    return pl.pallas_call(
        pack_kernel,
        out_shape=pltpu.VMEM((NCTX * IN_ROWS, LANES), F32),
        in_specs=[SMEM] + [HBM] * 5,
        out_specs=VMEM,
        scratch_shapes=[half] * 4
        + [
            pltpu.VMEM((BLOCK, LANES), F32),
            pltpu.VMEM((2, 2 * BLOCK, LANES), F32),
            pltpu.SemaphoreType.DMA((5,)),
        ],
        compiler_params=params(),
        cost_estimate=cost(1 << 20, 3 << 20),
        name="pack",
    )(plane, *in_hbm(q, k, v, g, f))


def lag_part(genome_blocks, plane, x, tables, g, c):
    return pl.pallas_call(
        lag_kernel,
        out_shape=[
            shape(PLANES, 4 * MOST, LANES),
            shape(NCTX + GAP * GENOMES, OWN, WIDE),
            pltpu.HBM(g.shape, BF16),
        ],
        in_specs=[SMEM] * 2 + [VMEM] * 5,
        out_specs=[VMEM, VMEM, HBM],
        scratch_shapes=[
            pltpu.VMEM((NCTX + UNROLL, OWN, WIDE), F32),
            pltpu.VMEM((MOST + TILE, OWN, WIDE), F32),
            pltpu.VMEM((2, OWN * MOST, LANES), F32),
            pltpu.VMEM(g.shape, BF16),
            pltpu.SemaphoreType.DMA(()),
        ],
        compiler_params=params(),
        cost_estimate=cost(1 << 36, 16 << 20),
        name="lag_part",
    )(genome_blocks, plane, x, *tables, g, c)


def back_part(genome_blocks, plane, carried, quarters, table):
    return pl.pallas_call(
        back_kernel,
        out_shape=shape(NCTX + TILE, OWN, WIDE),
        in_specs=[SMEM, SMEM] + [VMEM] * 6,
        out_specs=VMEM,
        scratch_shapes=[
            pltpu.VMEM((TILE - 1 + MOST + UNROLL, OWN, WIDE), F32),
            pltpu.VMEM((2, OWN * MOST, LANES), F32),
        ],
        compiler_params=params(),
        cost_estimate=cost(1 << 36, 16 << 20),
        name="back_part",
    )(genome_blocks, plane, carried, *quarters, table)


def finish(back, lags, table):
    return pl.pallas_call(
        finish_kernel,
        out_shape=pltpu.VMEM((NCTX * OUT_ROWS, LANES), F32),
        in_specs=[VMEM] * 6,
        out_specs=VMEM,
        compiler_params=params(),
        cost_estimate=cost(1 << 28, 4 << 20),
        name="finish",
    )(back, *lags, table)


def unpack(x, q, k, scale):
    half = pltpu.VMEM(q.shape, BF16)
    wide = pltpu.VMEM((BLOCK, LANES), F32)
    return pl.pallas_call(
        functools.partial(unpack_kernel, scale),
        out_shape=[pltpu.HBM(a.shape, a.dtype) for a in (half, half, wide)],
        in_specs=[VMEM] * 3,
        out_specs=[HBM] * 3,
        scratch_shapes=[
            half,
            half,
            wide,
            pltpu.VMEM((2, 2 * BLOCK, LANES), F32),
            pltpu.SemaphoreType.DMA((6,)),
        ],
        compiler_params=params(),
        cost_estimate=cost(1 << 20, 3 << 20),
        name="unpack",
    )(x, q, k)


def shift(x, k):
    return lax.ppermute(x, "ch", [(i, i ^ k) for i in range(PLANES)])


def exchange(x):
    return lax.all_to_all(x, "ctx", split_axis=0, concat_axis=0, tiled=True)


def local(q, k, v, g, c, filters, genome_blocks):
    forward, inverse = [jnp.asarray(t) for t in dft_tables()]
    plane = lax.axis_index("ch").astype(jnp.int32).reshape(1)
    sent = pack(plane, q, k, v, g, filters)
    got = exchange(sent.reshape(NCTX, IN_ROWS // 4, 4, LANES))
    own_quarter = got[:MOST, 8].reshape(4 * MOST, LANES)
    near, other = shift(own_quarter, 1), shift(own_quarter, 3)
    slots, carried, grad_value = lag_part(
        genome_blocks, plane, got.reshape(NCTX * IN_ROWS, LANES), (forward, inverse), g, c
    )
    slots, relayed = lax.optimization_barrier((slots, near))
    quarters = [own_quarter, near, shift(relayed, 3), other]
    lags = [slots[0]] + [shift(slots[i], i) for i in range(1, PLANES)]
    back = back_part(genome_blocks, plane, carried, quarters, forward)
    out = finish(back, lags, inverse).reshape(NCTX, OUT_ROWS // 4, 4, LANES)
    returned = exchange(out).reshape(NCTX * OUT_ROWS, LANES)
    scale = (NCTX * BLOCK) ** (-0.5)
    grad_query, grad_key, grad_filters = unpack(returned, q, k, scale)
    return grad_query, grad_key, grad_value, grad_filters


def solution(mesh):
    split = P("ctx", "ch")
    return jax.shard_map(
        local,
        mesh=mesh,
        in_specs=(split,) * 5 + (P("ctx", None), P()),
        out_specs=(split,) * 4,
        check_vma=False,
    )
```

```python
import functools

import jax
import jax.numpy as jnp
import ml_dtypes
import numpy as np
from jax import lax
from jax.experimental import pallas as pl
from jax.experimental.pallas import tpu as pltpu
from jax.sharding import PartitionSpec as P

BLOCK = 256
LANES = 128
OWN = 8
PLANES = 4
NCTX = 64
MOST = 32
GENOMES = 8
UNROLL = 4
TILE = 4
GAP = UNROLL + TILE - 2
WIDE = 3 * BLOCK
IN_ROWS = 36
OUT_ROWS = 20
F32 = jnp.float32
BF16 = jnp.bfloat16


def split_table(table):
    high = table.astype(ml_dtypes.bfloat16)
    low = (table - high.astype(np.float64)).astype(ml_dtypes.bfloat16)
    return np.concatenate([high, low, high], axis=0)


def dft_tables():
    freq = np.arange(BLOCK)
    sample = np.arange(BLOCK)
    phase = (sample[:, None] * (2 * freq[None, :] + 1)) % (4 * BLOCK)
    angle = phase * (np.pi / (2 * BLOCK))
    forward = np.concatenate([np.cos(angle), -np.sin(angle)], axis=1)
    return split_table(forward), split_table(forward.T / BLOCK)


def dot3(x, table):
    high = x.astype(BF16)
    low = (x - high.astype(F32)).astype(BF16)
    left = jnp.concatenate([low, high, high], 1)
    parts = [
        jnp.dot(left, table[:, i : i + BLOCK], preferred_element_type=F32)
        for i in range(0, table.shape[1], BLOCK)
    ]
    return jnp.concatenate(parts, 1) if len(parts) > 1 else parts[0]


def pack_kernel(
    plane_ref, here_ref, q_hbm, k_hbm, v_hbm, g_hbm, f_hbm, out_ref, q_ref, k_ref, v_ref, g_ref, f_ref,
    turned, sems,
):
    column = pl.multiple_of(plane_ref[0] * LANES, LANES)
    pairs = (
        (g_hbm, g_ref), (v_hbm, v_ref), (q_hbm, q_ref), (k_hbm, k_ref),
        (f_hbm.at[:, pl.ds(column, LANES)], f_ref),
    )
    copies = [pltpu.make_async_copy(a, b, sems.at[i]) for i, (a, b) in enumerate(pairs)]

    @pl.when(here_ref[0] < MOST)
    def _():
        copies[4].start()
        for copy in copies[:4]:
            copy.start()
        copies[4].wait()
        for half in range(2):
            turned[half, 0:LANES, :] = f_ref[half * LANES : (half + 1) * LANES, :].T
            for r in range(2):
                rows = turned[half, pl.ds(r, NCTX, stride=2), :]
                out_ref[pl.ds(32 + 2 * half + r, NCTX, stride=IN_ROWS), :] = rows

    @pl.when(here_ref[0] >= MOST)
    def _():
        for copy in copies[:4]:
            copy.start()
        for i in range(NCTX):
            out_ref[IN_ROWS * i + 32 : IN_ROWS * i + 36, :] = jnp.zeros((4, LANES), F32)

    for which, (a_ref, b_ref, first_copy) in enumerate(((g_ref, v_ref, 0), (q_ref, k_ref, 2))):
        copies[first_copy].wait()
        copies[first_copy + 1].wait()
        product = a_ref[...].astype(F32) * b_ref[...].astype(F32)
        for half in range(2):
            turned[half] = product[half * LANES : (half + 1) * LANES, :].T
        for half in range(2):
            for quarter in range(PLANES):
                for r in range(2):
                    rows = turned[half, pl.ds(LANES * quarter + r, NCTX, stride=2), :]
                    first = 16 * (1 - which) + 8 * half + 2 * quarter + r
                    out_ref[pl.ds(first, NCTX, stride=IN_ROWS), :] = rows


def signs():
    lane = lax.broadcasted_iota(jnp.int32, (1, BLOCK), 1)
    return (1 - 2 * (lane % 2)).astype(F32)


def add_pairs(totals, pairs, first, second, halves=(0, 1), fresh=False):
    for half in halves:
        loaded = {}

        def load(name, view, index):
            if (name, index) not in loaded:
                loaded[name, index] = [
                    view[index, :, pl.ds(BLOCK * i + LANES * half, LANES)] for i in range(3)
                ]
            return loaded[name, index]

        out = {}
        for j, index, other in pairs:
            a, b = load("first", first, index), load("second", second, other)
            for i in range(3):
                lanes = pl.ds(BLOCK * i + LANES * half, LANES)
                if (j, i) not in out and not fresh:
                    out[j, i] = totals[j, :, lanes]
                product = a[i] * b[i]
                out[j, i] = out[j, i] + product if (j, i) in out else product
        for (j, i), value in out.items():
            totals[j, :, pl.ds(BLOCK * i + LANES * half, LANES)] = value


def alone(count, function, *args):
    def body(_, carry):
        function(*args)
        return carry

    lax.fori_loop(0, count // MOST, body, 0)


def lag_kernel(
    genome_ref, plane_ref, x_ref, fwd_ref, inv_ref, g_ref, c_ref,
    lag_ref, carried_ref, value_hbm, gated, lags, flat, value_ref, sem,
):
    value_ref[...] = (g_ref[...].astype(F32) * c_ref[...].astype(F32)).astype(BF16)
    give = pltpu.make_async_copy(value_ref, value_hbm, sem)
    give.start()
    end = jnp.int32(0)
    for g in range(GENOMES):
        end = end + genome_ref[g]
        carried_ref[pl.ds(end + GAP * g, GAP)] = jnp.zeros((GAP, OWN, WIDE), F32)
    lags[...] = jnp.zeros_like(lags)
    gated[NCTX:] = jnp.zeros((UNROLL, OWN, WIDE), F32)
    places, own, end = [], jnp.int32(0), genome_ref[0]
    for s in range(NCTX):
        if s:
            own = own + (s >= end).astype(jnp.int32)
            end = jnp.where(s >= end, end + genome_ref[own], end)
        places.append(s + GAP * own)
    group = 32
    for part in range(NCTX // group):
        rows = []
        for which in range(2):
            for s in range(part * group, (part + 1) * group):
                base = IN_ROWS * s + 16 * which
                rows.append(
                    jnp.concatenate([x_ref[base : base + 8, :], x_ref[base + 8 : base + 16, :]], 1)
                )
        spec = dot3(jnp.concatenate(rows, 0), fwd_ref).reshape(2, group, OWN, 2 * BLOCK)
        re, im = spec[0, :, :, :BLOCK], spec[0, :, :, BLOCK:]
        blocks = pl.ds(group * part, group)
        gated[blocks, :, 0:BLOCK] = re - im
        gated[blocks, :, BLOCK : 2 * BLOCK] = re
        gated[blocks, :, 2 * BLOCK : WIDE] = im
        re, im = spec[1, :, :, :BLOCK], spec[1, :, :, BLOCK:]
        less, more = im - re, re + im
        for i in range(group):
            block = places[part * group + i]
            carried_ref[block, :, 0:BLOCK] = re[i]
            carried_ref[block, :, BLOCK : 2 * BLOCK] = less[i]
            carried_ref[block, :, 2 * BLOCK : WIDE] = more[i]
    pairs = [(j, u, u + j) for u in range(UNROLL) for j in range(TILE)]

    def genome(g, begin):
        count = genome_ref[g]
        first = begin + GAP * g

        def tile(i, _):
            d = TILE * i

            totals = lags.at[pl.ds(d, TILE)]

            def step(c, _):
                s = UNROLL * c
                here = gated.at[pl.ds(begin + s, UNROLL)]
                after = carried_ref.at[pl.ds(first + d + s, UNROLL + TILE - 1)]
                add_pairs(totals, pairs, here, after)
                return 0

            lax.fori_loop(0, (count - d + UNROLL - 1) // UNROLL, step, 0)
            return 0

        lax.fori_loop(0, (count + TILE - 1) // TILE, tile, 0)
        return begin + count

    lax.fori_loop(0, GENOMES, genome, jnp.int32(0))
    sign = signs()
    k1, k2, k3 = [
        lags[: MOST + 1, :, BLOCK * i : BLOCK * (i + 1)].reshape(OWN * (MOST + 1), BLOCK)
        for i in range(3)
    ]
    re, im = k1 + k3, k1 + k2
    spec = jnp.concatenate(
        [re[: OWN * MOST] + sign * im[OWN:], im[: OWN * MOST] - sign * re[OWN:]], 1
    )
    for part in range(2):
        top = OWN * MOST // 2 * part
        rows = dot3(spec[top : top + OWN * MOST // 2, :], inv_ref)
        for half in range(2):
            flat[half, top : top + OWN * MOST // 2, :] = rows[
                :, half * LANES : (half + 1) * LANES
            ]
    for quarter in range(PLANES):
        slot = lax.bitwise_xor(jnp.int32(quarter), plane_ref[0])
        for half in range(2):
            for r in range(2):
                rows = flat[half, pl.ds(2 * quarter + r, MOST, stride=OWN), :]
                lag_ref[slot, pl.ds(2 * half + r, MOST, stride=4), :] = rows
    give.wait()


def back_kernel(
    genome_ref, plane_ref, carried_ref, f0_ref, f1_ref, f2_ref, f3_ref, fwd_ref, back, filt, flat,
):
    for k, f_ref in enumerate((f0_ref, f1_ref, f2_ref, f3_ref)):
        quarter = lax.bitwise_xor(jnp.int32(k), plane_ref[0])
        for half in range(2):
            for r in range(2):
                rows = f_ref[pl.ds(2 * half + r, MOST, stride=4), :]
                flat[half, pl.ds(2 * quarter + r, MOST, stride=OWN), :] = rows
    spec = dot3(jnp.concatenate([flat[0], flat[1]], 1), fwd_ref)
    sign = signs()
    prior = jnp.concatenate([jnp.zeros((OWN, 2 * BLOCK), F32), spec[: OWN * (MOST - 1), :]], 0)
    re = spec[:, :BLOCK] - sign * prior[:, BLOCK:]
    im = spec[:, BLOCK:] + sign * prior[:, :BLOCK]
    head = TILE - 1
    filt[:head] = jnp.zeros((head, OWN, WIDE), F32)
    for i, value in enumerate((re - im, re, im)):
        filt[head : head + MOST, :, BLOCK * i : BLOCK * (i + 1)] = value.reshape(MOST, OWN, BLOCK)
    filt[head + MOST :] = jnp.zeros((UNROLL, OWN, WIDE), F32)
    pairs = [(j, u - j + head, u) for u in range(UNROLL) for j in range(TILE)]

    def genome(g, begin):
        count = genome_ref[g]
        first = begin + GAP * g

        @pl.when(count == MOST)
        def _():
            taps, later = filt.at[head : head + MOST], carried_ref.at[pl.ds(first, MOST)]
            for b in range(0, MOST, TILE):
                every = [
                    (j, t - b - j, t)
                    for t in range(b, MOST)
                    for j in range(TILE)
                    if t >= b + j
                ]
                rows = back.at[pl.ds(begin + b, TILE)]
                for half in range(2):
                    alone(count, add_pairs, rows, every, taps, later, (half,), True)

        def tile(i, _):
            b = TILE * i

            totals = back.at[pl.ds(begin + b, TILE)]
            totals[...] = jnp.zeros((TILE, OWN, WIDE), F32)

            def step(c, _):
                t = UNROLL * c
                taps = filt.at[pl.ds(t, UNROLL + TILE - 1)]
                later = carried_ref.at[pl.ds(first + b + t, UNROLL)]
                add_pairs(totals, pairs, taps, later)
                return 0

            lax.fori_loop(0, (count - b + UNROLL - 1) // UNROLL, step, 0)
            return 0

        tiles = jnp.where(count == MOST, 0, (count + TILE - 1) // TILE)
        lax.fori_loop(0, tiles, tile, 0)
        return begin + count

    lax.fori_loop(0, GENOMES, genome, jnp.int32(0))


def finish_kernel(back, l0_ref, l1_ref, l2_ref, l3_ref, inv_ref, out_ref):
    group = 32
    for part in range(NCTX // group):
        k1, k2, k3 = [
            back[group * part : group * (part + 1), :, BLOCK * i : BLOCK * (i + 1)].reshape(
                OWN * group, BLOCK
            )
            for i in range(3)
        ]
        rows = dot3(jnp.concatenate([k1 + k3, k1 + k2], 1), inv_ref)
        for i in range(group):
            base = OUT_ROWS * (part * group + i)
            for half in range(2):
                out_ref[base + 8 * half : base + 8 * half + 8, :] = rows[
                    OWN * i : OWN * (i + 1), half * LANES : (half + 1) * LANES
                ]
    for i in range(MOST):
        part = slice(4 * i, 4 * i + 4)
        total = (l0_ref[part, :] + l1_ref[part, :]) + (l2_ref[part, :] + l3_ref[part, :])
        out_ref[OUT_ROWS * i + 16 : OUT_ROWS * i + 20, :] = total
    for i in range(MOST, NCTX):
        out_ref[OUT_ROWS * i + 16 : OUT_ROWS * i + 20, :] = jnp.zeros((4, LANES), F32)


def unpack_kernel(
    scale, x_ref, q_ref, k_ref, gq_hbm, gk_hbm, gf_hbm, gq_ref, gk_ref, gf_ref, turned, sems
):
    copies = []

    def send(source, target, rows):
        copy = pltpu.make_async_copy(source.at[rows], target.at[rows], sems.at[len(copies)])
        copy.start()
        copies.append(copy)

    for half in range(2):
        for quarter in range(PLANES):
            for r in range(2):
                rows = x_ref[pl.ds(8 * half + 2 * quarter + r, NCTX, stride=OUT_ROWS), :]
                turned[half, pl.ds(LANES * quarter + r, NCTX, stride=2), :] = rows
        part = pl.ds(half * LANES, LANES)
        back = turned[half].T
        gq_ref[part, :] = (back * k_ref[part, :].astype(F32)).astype(BF16)
        send(gq_ref, gq_hbm, part)
        gk_ref[part, :] = (back * q_ref[part, :].astype(F32)).astype(BF16)
        send(gk_ref, gk_hbm, part)
        for r in range(2):
            rows = x_ref[pl.ds(16 + 2 * half + r, NCTX, stride=OUT_ROWS), :]
            turned[half, pl.ds(r, NCTX, stride=2), :] = rows
        gf_ref[part, :] = turned[half, 0:LANES, :].T * scale
        send(gf_ref, gf_hbm, part)
    for copy in copies:
        copy.wait()


VMEM = pl.BlockSpec(memory_space=pltpu.VMEM)
SMEM = pl.BlockSpec(memory_space=pltpu.SMEM)
HBM = pl.BlockSpec(memory_space=pltpu.HBM)


def params(mib=40):
    return pltpu.CompilerParams(vmem_limit_bytes=mib * 1024 * 1024)


def cost(flops, moved):
    return pl.CostEstimate(flops=flops, bytes_accessed=moved, transcendentals=0)


def shape(*dims):
    return jax.ShapeDtypeStruct(dims, F32)


def in_hbm(*arrays):
    return [pltpu.with_memory_space_constraint(a, pltpu.HBM) for a in arrays]


def pack(plane, here, q, k, v, g, f):
    half = pltpu.VMEM(q.shape, BF16)
    return pl.pallas_call(
        pack_kernel,
        out_shape=pltpu.VMEM((NCTX * IN_ROWS, LANES), F32),
        in_specs=[SMEM] * 2 + [HBM] * 5,
        out_specs=VMEM,
        scratch_shapes=[half] * 4
        + [
            pltpu.VMEM((BLOCK, LANES), F32),
            pltpu.VMEM((2, 2 * BLOCK, LANES), F32),
            pltpu.SemaphoreType.DMA((5,)),
        ],
        compiler_params=params(),
        cost_estimate=cost(1 << 20, 3 << 20),
        name="pack",
    )(plane, here, *in_hbm(q, k, v, g, f))


def lag_part(genome_blocks, plane, x, tables, g, c):
    return pl.pallas_call(
        lag_kernel,
        out_shape=[
            shape(PLANES, 4 * MOST, LANES),
            shape(NCTX + GAP * GENOMES, OWN, WIDE),
            pltpu.HBM(g.shape, BF16),
        ],
        in_specs=[SMEM] * 2 + [VMEM] * 5,
        out_specs=[VMEM, VMEM, HBM],
        scratch_shapes=[
            pltpu.VMEM((NCTX + UNROLL, OWN, WIDE), F32),
            pltpu.VMEM((MOST + TILE, OWN, WIDE), F32),
            pltpu.VMEM((2, OWN * MOST, LANES), F32),
            pltpu.VMEM(g.shape, BF16),
            pltpu.SemaphoreType.DMA(()),
        ],
        compiler_params=params(),
        cost_estimate=cost(1 << 36, 16 << 20),
        name="lag_part",
    )(genome_blocks, plane, x, *tables, g, c)


def back_part(genome_blocks, plane, carried, quarters, table):
    return pl.pallas_call(
        back_kernel,
        out_shape=shape(NCTX + TILE, OWN, WIDE),
        in_specs=[SMEM, SMEM] + [VMEM] * 6,
        out_specs=VMEM,
        scratch_shapes=[
            pltpu.VMEM((TILE - 1 + MOST + UNROLL, OWN, WIDE), F32),
            pltpu.VMEM((2, OWN * MOST, LANES), F32),
        ],
        compiler_params=params(),
        cost_estimate=cost(1 << 36, 16 << 20),
        name="back_part",
    )(genome_blocks, plane, carried, *quarters, table)


def finish(back, lags, table):
    return pl.pallas_call(
        finish_kernel,
        out_shape=pltpu.VMEM((NCTX * OUT_ROWS, LANES), F32),
        in_specs=[VMEM] * 6,
        out_specs=VMEM,
        compiler_params=params(),
        cost_estimate=cost(1 << 28, 4 << 20),
        name="finish",
    )(back, *lags, table)


def unpack(x, q, k, scale):
    half = pltpu.VMEM(q.shape, BF16)
    wide = pltpu.VMEM((BLOCK, LANES), F32)
    return pl.pallas_call(
        functools.partial(unpack_kernel, scale),
        out_shape=[pltpu.HBM(a.shape, a.dtype) for a in (half, half, wide)],
        in_specs=[VMEM] * 3,
        out_specs=[HBM] * 3,
        scratch_shapes=[
            half,
            half,
            wide,
            pltpu.VMEM((2, 2 * BLOCK, LANES), F32),
            pltpu.SemaphoreType.DMA((6,)),
        ],
        compiler_params=params(),
        cost_estimate=cost(1 << 20, 3 << 20),
        name="unpack",
    )(x, q, k)


def shift(x, k):
    return lax.ppermute(x, "ch", [(i, i ^ k) for i in range(PLANES)])


def exchange(x):
    return lax.all_to_all(x, "ctx", split_axis=0, concat_axis=0, tiled=True)


def local(q, k, v, g, c, filters, genome_blocks):
    forward, inverse = [jnp.asarray(t) for t in dft_tables()]
    plane = lax.axis_index("ch").astype(jnp.int32).reshape(1)
    here = lax.axis_index("ctx").astype(jnp.int32).reshape(1)
    sent = pack(plane, here, q, k, v, g, filters)
    got = exchange(sent.reshape(NCTX, IN_ROWS // 4, 4, LANES))
    own_quarter = got[:MOST, 8].reshape(4 * MOST, LANES)
    near, other = shift(own_quarter, 1), shift(own_quarter, 3)
    slots, carried, grad_value = lag_part(
        genome_blocks, plane, got.reshape(NCTX * IN_ROWS, LANES), (forward, inverse), g, c
    )
    slots, relayed = lax.optimization_barrier((slots, other))
    quarters = [own_quarter, near, shift(relayed, 1), other]
    lags = [slots[0]] + [shift(slots[i], i) for i in range(1, PLANES)]
    back = back_part(genome_blocks, plane, carried, quarters, forward)
    out = finish(back, lags, inverse).reshape(NCTX, OUT_ROWS // 4, 4, LANES)
    returned = exchange(out).reshape(NCTX * OUT_ROWS, LANES)
    scale = (NCTX * BLOCK) ** (-0.5)
    grad_query, grad_key, grad_filters = unpack(returned, q, k, scale)
    return grad_query, grad_key, grad_value, grad_filters


def solution(mesh):
    split = P("ctx", "ch")
    return jax.shard_map(
        local,
        mesh=mesh,
        in_specs=(split,) * 5 + (P("ctx", None), P()),
        out_specs=(split,) * 4,
        check_vma=False,
    )
```

```python
import functools

import jax
import jax.numpy as jnp
import ml_dtypes
import numpy as np
from jax import lax
from jax.experimental import pallas as pl
from jax.experimental.pallas import tpu as pltpu
from jax.sharding import PartitionSpec as P

BLOCK = 256
LANES = 128
OWN = 8
PLANES = 4
NCTX = 64
MOST = 32
GENOMES = 8
UNROLL = 4
TILE = 4
GAP = UNROLL + TILE - 2
WIDE = 3 * BLOCK
IN_ROWS = 36
OUT_ROWS = 20
F32 = jnp.float32
BF16 = jnp.bfloat16


def split_table(table):
    high = table.astype(ml_dtypes.bfloat16)
    low = (table - high.astype(np.float64)).astype(ml_dtypes.bfloat16)
    return np.concatenate([high, low, high], axis=0)


def dft_tables():
    freq = np.arange(BLOCK)
    sample = np.arange(BLOCK)
    phase = (sample[:, None] * (2 * freq[None, :] + 1)) % (4 * BLOCK)
    angle = phase * (np.pi / (2 * BLOCK))
    forward = np.concatenate([np.cos(angle), -np.sin(angle)], axis=1)
    return split_table(forward), split_table(forward.T / BLOCK)


def dot3(x, table):
    high = x.astype(BF16)
    low = (x - high.astype(F32)).astype(BF16)
    left = jnp.concatenate([low, high, high], 1)
    parts = [
        jnp.dot(left, table[:, i : i + BLOCK], preferred_element_type=F32)
        for i in range(0, table.shape[1], BLOCK)
    ]
    return jnp.concatenate(parts, 1) if len(parts) > 1 else parts[0]


def pack_kernel(
    plane_ref, here_ref, q_hbm, k_hbm, v_hbm, g_hbm, f_hbm, out_ref, q_ref, k_ref, v_ref, g_ref, f_ref,
    turned, sems,
):
    column = pl.multiple_of(plane_ref[0] * LANES, LANES)
    pairs = (
        (g_hbm, g_ref), (v_hbm, v_ref), (q_hbm, q_ref), (k_hbm, k_ref),
        (f_hbm.at[:, pl.ds(column, LANES)], f_ref),
    )
    copies = [pltpu.make_async_copy(a, b, sems.at[i]) for i, (a, b) in enumerate(pairs)]

    @pl.when(here_ref[0] < MOST)
    def _():
        copies[4].start()
        for copy in copies[:4]:
            copy.start()
        copies[4].wait()
        for half in range(2):
            turned[half, 0:LANES, :] = f_ref[half * LANES : (half + 1) * LANES, :].T
            for r in range(2):
                rows = turned[half, pl.ds(r, NCTX, stride=2), :]
                out_ref[pl.ds(32 + 2 * half + r, NCTX, stride=IN_ROWS), :] = rows

    @pl.when(here_ref[0] >= MOST)
    def _():
        for copy in copies[:4]:
            copy.start()
        for i in range(NCTX):
            out_ref[IN_ROWS * i + 32 : IN_ROWS * i + 36, :] = jnp.zeros((4, LANES), F32)

    for which, (a_ref, b_ref, first_copy) in enumerate(((g_ref, v_ref, 0), (q_ref, k_ref, 2))):
        copies[first_copy].wait()
        copies[first_copy + 1].wait()
        product = a_ref[...].astype(F32) * b_ref[...].astype(F32)
        for half in range(2):
            turned[half] = product[half * LANES : (half + 1) * LANES, :].T
        for half in range(2):
            for quarter in range(PLANES):
                for r in range(2):
                    rows = turned[half, pl.ds(LANES * quarter + r, NCTX, stride=2), :]
                    first = 16 * (1 - which) + 8 * half + 2 * quarter + r
                    out_ref[pl.ds(first, NCTX, stride=IN_ROWS), :] = rows


def signs():
    lane = lax.broadcasted_iota(jnp.int32, (1, BLOCK), 1)
    return (1 - 2 * (lane % 2)).astype(F32)


def add_pairs(totals, pairs, first, second, halves=(0, 1), fresh=False):
    for half in halves:
        loaded = {}

        def load(name, view, index):
            if (name, index) not in loaded:
                loaded[name, index] = [
                    view[index, :, pl.ds(BLOCK * i + LANES * half, LANES)] for i in range(3)
                ]
            return loaded[name, index]

        out = {}
        for j, index, other in pairs:
            a, b = load("first", first, index), load("second", second, other)
            for i in range(3):
                lanes = pl.ds(BLOCK * i + LANES * half, LANES)
                if (j, i) not in out and not fresh:
                    out[j, i] = totals[j, :, lanes]
                product = a[i] * b[i]
                out[j, i] = out[j, i] + product if (j, i) in out else product
        for (j, i), value in out.items():
            totals[j, :, pl.ds(BLOCK * i + LANES * half, LANES)] = value


def alone(count, function, *args):
    def body(_, carry):
        function(*args)
        return carry

    lax.fori_loop(0, count // MOST, body, 0)


def lag_kernel(
    genome_ref, plane_ref, x_ref, fwd_ref, inv_ref, g_ref, c_ref,
    lag_ref, carried_ref, value_hbm, gated, lags, flat, value_ref, sem,
):
    value_ref[...] = (g_ref[...].astype(F32) * c_ref[...].astype(F32)).astype(BF16)
    give = pltpu.make_async_copy(value_ref, value_hbm, sem)
    give.start()
    end = jnp.int32(0)
    for g in range(GENOMES):
        end = end + genome_ref[g]
        carried_ref[pl.ds(end + GAP * g, GAP)] = jnp.zeros((GAP, OWN, WIDE), F32)
    lags[...] = jnp.zeros_like(lags)
    gated[NCTX:] = jnp.zeros((UNROLL, OWN, WIDE), F32)
    places, own, end = [], jnp.int32(0), genome_ref[0]
    for s in range(NCTX):
        if s:
            own = own + (s >= end).astype(jnp.int32)
            end = jnp.where(s >= end, end + genome_ref[own], end)
        places.append(s + GAP * own)
    group = 32
    for part in range(NCTX // group):
        rows = []
        for which in range(2):
            for s in range(part * group, (part + 1) * group):
                base = IN_ROWS * s + 16 * which
                rows.append(
                    jnp.concatenate([x_ref[base : base + 8, :], x_ref[base + 8 : base + 16, :]], 1)
                )
        spec = dot3(jnp.concatenate(rows, 0), fwd_ref).reshape(2, group, OWN, 2 * BLOCK)
        re, im = spec[0, :, :, :BLOCK], spec[0, :, :, BLOCK:]
        blocks = pl.ds(group * part, group)
        gated[blocks, :, 0:BLOCK] = re - im
        gated[blocks, :, BLOCK : 2 * BLOCK] = re
        gated[blocks, :, 2 * BLOCK : WIDE] = im
        re, im = spec[1, :, :, :BLOCK], spec[1, :, :, BLOCK:]
        less, more = im - re, re + im
        for i in range(group):
            block = places[part * group + i]
            carried_ref[block, :, 0:BLOCK] = re[i]
            carried_ref[block, :, BLOCK : 2 * BLOCK] = less[i]
            carried_ref[block, :, 2 * BLOCK : WIDE] = more[i]
    pairs = [(j, u, u + j) for u in range(UNROLL) for j in range(TILE)]

    def genome(g, begin):
        count = genome_ref[g]
        first = begin + GAP * g

        def tile(i, _):
            d = TILE * i

            totals = lags.at[pl.ds(d, TILE)]

            def step(c, _):
                s = UNROLL * c
                here = gated.at[pl.ds(begin + s, UNROLL)]
                after = carried_ref.at[pl.ds(first + d + s, UNROLL + TILE - 1)]
                add_pairs(totals, pairs, here, after)
                return 0

            lax.fori_loop(0, (count - d + UNROLL - 1) // UNROLL, step, 0)
            return 0

        lax.fori_loop(0, (count + TILE - 1) // TILE, tile, 0)
        return begin + count

    lax.fori_loop(0, GENOMES, genome, jnp.int32(0))
    sign = signs()
    k1, k2, k3 = [
        lags[: MOST + 1, :, BLOCK * i : BLOCK * (i + 1)].reshape(OWN * (MOST + 1), BLOCK)
        for i in range(3)
    ]
    re, im = k1 + k3, k1 + k2
    spec = jnp.concatenate(
        [re[: OWN * MOST] + sign * im[OWN:], im[: OWN * MOST] - sign * re[OWN:]], 1
    )
    for part in range(2):
        top = OWN * MOST // 2 * part
        rows = dot3(spec[top : top + OWN * MOST // 2, :], inv_ref)
        for half in range(2):
            flat[half, top : top + OWN * MOST // 2, :] = rows[
                :, half * LANES : (half + 1) * LANES
            ]
    for quarter in range(PLANES):
        slot = lax.bitwise_xor(jnp.int32(quarter), plane_ref[0])
        for half in range(2):
            for r in range(2):
                rows = flat[half, pl.ds(2 * quarter + r, MOST, stride=OWN), :]
                lag_ref[slot, pl.ds(2 * half + r, MOST, stride=4), :] = rows
    give.wait()


def back_kernel(
    genome_ref, plane_ref, carried_ref, own_ref, near_ref, both_ref, fwd_ref, back, filt, flat,
):
    sources = ((own_ref, 0), (both_ref, 0), (both_ref, 4 * MOST), (near_ref, 0))
    for k, (f_ref, top) in enumerate(sources):
        quarter = lax.bitwise_xor(jnp.int32(k), plane_ref[0])
        for half in range(2):
            for r in range(2):
                rows = f_ref[pl.ds(top + 2 * half + r, MOST, stride=4), :]
                flat[half, pl.ds(2 * quarter + r, MOST, stride=OWN), :] = rows
    spec = dot3(jnp.concatenate([flat[0], flat[1]], 1), fwd_ref)
    sign = signs()
    prior = jnp.concatenate([jnp.zeros((OWN, 2 * BLOCK), F32), spec[: OWN * (MOST - 1), :]], 0)
    re = spec[:, :BLOCK] - sign * prior[:, BLOCK:]
    im = spec[:, BLOCK:] + sign * prior[:, :BLOCK]
    head = TILE - 1
    filt[:head] = jnp.zeros((head, OWN, WIDE), F32)
    for i, value in enumerate((re - im, re, im)):
        filt[head : head + MOST, :, BLOCK * i : BLOCK * (i + 1)] = value.reshape(MOST, OWN, BLOCK)
    filt[head + MOST :] = jnp.zeros((UNROLL, OWN, WIDE), F32)
    pairs = [(j, u - j + head, u) for u in range(UNROLL) for j in range(TILE)]

    def genome(g, begin):
        count = genome_ref[g]
        first = begin + GAP * g

        @pl.when(count == MOST)
        def _():
            taps, later = filt.at[head : head + MOST], carried_ref.at[pl.ds(first, MOST)]
            for b in range(0, MOST, TILE):
                every = [
                    (j, t - b - j, t)
                    for t in range(b, MOST)
                    for j in range(TILE)
                    if t >= b + j
                ]
                rows = back.at[pl.ds(begin + b, TILE)]
                for half in range(2):
                    alone(count, add_pairs, rows, every, taps, later, (half,), True)

        def tile(i, _):
            b = TILE * i

            totals = back.at[pl.ds(begin + b, TILE)]
            totals[...] = jnp.zeros((TILE, OWN, WIDE), F32)

            def step(c, _):
                t = UNROLL * c
                taps = filt.at[pl.ds(t, UNROLL + TILE - 1)]
                later = carried_ref.at[pl.ds(first + b + t, UNROLL)]
                add_pairs(totals, pairs, taps, later)
                return 0

            lax.fori_loop(0, (count - b + UNROLL - 1) // UNROLL, step, 0)
            return 0

        tiles = jnp.where(count == MOST, 0, (count + TILE - 1) // TILE)
        lax.fori_loop(0, tiles, tile, 0)
        return begin + count

    lax.fori_loop(0, GENOMES, genome, jnp.int32(0))


def finish_kernel(back, l0_ref, l1_ref, l2_ref, l3_ref, inv_ref, out_ref):
    group = 32
    for part in range(NCTX // group):
        k1, k2, k3 = [
            back[group * part : group * (part + 1), :, BLOCK * i : BLOCK * (i + 1)].reshape(
                OWN * group, BLOCK
            )
            for i in range(3)
        ]
        rows = dot3(jnp.concatenate([k1 + k3, k1 + k2], 1), inv_ref)
        for i in range(group):
            base = OUT_ROWS * (part * group + i)
            for half in range(2):
                out_ref[base + 8 * half : base + 8 * half + 8, :] = rows[
                    OWN * i : OWN * (i + 1), half * LANES : (half + 1) * LANES
                ]
    for i in range(MOST):
        part = slice(4 * i, 4 * i + 4)
        total = (l0_ref[part, :] + l1_ref[part, :]) + (l2_ref[part, :] + l3_ref[part, :])
        out_ref[OUT_ROWS * i + 16 : OUT_ROWS * i + 20, :] = total
    for i in range(MOST, NCTX):
        out_ref[OUT_ROWS * i + 16 : OUT_ROWS * i + 20, :] = jnp.zeros((4, LANES), F32)


def unpack_kernel(
    scale, x_ref, q_ref, k_ref, gq_hbm, gk_hbm, gf_hbm, gq_ref, gk_ref, gf_ref, turned, sems
):
    copies = []

    def send(source, target, rows):
        copy = pltpu.make_async_copy(source.at[rows], target.at[rows], sems.at[len(copies)])
        copy.start()
        copies.append(copy)

    for half in range(2):
        for quarter in range(PLANES):
            for r in range(2):
                rows = x_ref[pl.ds(8 * half + 2 * quarter + r, NCTX, stride=OUT_ROWS), :]
                turned[half, pl.ds(LANES * quarter + r, NCTX, stride=2), :] = rows
        part = pl.ds(half * LANES, LANES)
        back = turned[half].T
        gq_ref[part, :] = (back * k_ref[part, :].astype(F32)).astype(BF16)
        send(gq_ref, gq_hbm, part)
        gk_ref[part, :] = (back * q_ref[part, :].astype(F32)).astype(BF16)
        send(gk_ref, gk_hbm, part)
        for r in range(2):
            rows = x_ref[pl.ds(16 + 2 * half + r, NCTX, stride=OUT_ROWS), :]
            turned[half, pl.ds(r, NCTX, stride=2), :] = rows
        gf_ref[part, :] = turned[half, 0:LANES, :].T * scale
        send(gf_ref, gf_hbm, part)
    for copy in copies:
        copy.wait()


VMEM = pl.BlockSpec(memory_space=pltpu.VMEM)
SMEM = pl.BlockSpec(memory_space=pltpu.SMEM)
HBM = pl.BlockSpec(memory_space=pltpu.HBM)


def params(mib=40):
    return pltpu.CompilerParams(vmem_limit_bytes=mib * 1024 * 1024)


def cost(flops, moved):
    return pl.CostEstimate(flops=flops, bytes_accessed=moved, transcendentals=0)


def shape(*dims):
    return jax.ShapeDtypeStruct(dims, F32)


def in_hbm(*arrays):
    return [pltpu.with_memory_space_constraint(a, pltpu.HBM) for a in arrays]


def pack(plane, here, q, k, v, g, f):
    half = pltpu.VMEM(q.shape, BF16)
    return pl.pallas_call(
        pack_kernel,
        out_shape=pltpu.VMEM((NCTX * IN_ROWS, LANES), F32),
        in_specs=[SMEM] * 2 + [HBM] * 5,
        out_specs=VMEM,
        scratch_shapes=[half] * 4
        + [
            pltpu.VMEM((BLOCK, LANES), F32),
            pltpu.VMEM((2, 2 * BLOCK, LANES), F32),
            pltpu.SemaphoreType.DMA((5,)),
        ],
        compiler_params=params(),
        cost_estimate=cost(1 << 20, 3 << 20),
        name="pack",
    )(plane, here, *in_hbm(q, k, v, g, f))


def lag_part(genome_blocks, plane, x, tables, g, c):
    return pl.pallas_call(
        lag_kernel,
        out_shape=[
            shape(PLANES, 4 * MOST, LANES),
            shape(NCTX + GAP * GENOMES, OWN, WIDE),
            pltpu.HBM(g.shape, BF16),
        ],
        in_specs=[SMEM] * 2 + [VMEM] * 5,
        out_specs=[VMEM, VMEM, HBM],
        scratch_shapes=[
            pltpu.VMEM((NCTX + UNROLL, OWN, WIDE), F32),
            pltpu.VMEM((MOST + TILE, OWN, WIDE), F32),
            pltpu.VMEM((2, OWN * MOST, LANES), F32),
            pltpu.VMEM(g.shape, BF16),
            pltpu.SemaphoreType.DMA(()),
        ],
        compiler_params=params(),
        cost_estimate=cost(1 << 36, 16 << 20),
        name="lag_part",
    )(genome_blocks, plane, x, *tables, g, c)


def back_part(genome_blocks, plane, carried, own, near, both, table):
    return pl.pallas_call(
        back_kernel,
        out_shape=shape(NCTX + TILE, OWN, WIDE),
        in_specs=[SMEM, SMEM] + [VMEM] * 5,
        out_specs=VMEM,
        scratch_shapes=[
            pltpu.VMEM((TILE - 1 + MOST + UNROLL, OWN, WIDE), F32),
            pltpu.VMEM((2, OWN * MOST, LANES), F32),
        ],
        compiler_params=params(),
        cost_estimate=cost(1 << 36, 16 << 20),
        name="back_part",
    )(genome_blocks, plane, carried, own, near, both, table)


def finish(back, lags, table):
    return pl.pallas_call(
        finish_kernel,
        out_shape=pltpu.VMEM((NCTX * OUT_ROWS, LANES), F32),
        in_specs=[VMEM] * 6,
        out_specs=VMEM,
        compiler_params=params(),
        cost_estimate=cost(1 << 28, 4 << 20),
        name="finish",
    )(back, *lags, table)


def unpack(x, q, k, scale):
    half = pltpu.VMEM(q.shape, BF16)
    wide = pltpu.VMEM((BLOCK, LANES), F32)
    return pl.pallas_call(
        functools.partial(unpack_kernel, scale),
        out_shape=[pltpu.HBM(a.shape, a.dtype) for a in (half, half, wide)],
        in_specs=[VMEM] * 3,
        out_specs=[HBM] * 3,
        scratch_shapes=[
            half,
            half,
            wide,
            pltpu.VMEM((2, 2 * BLOCK, LANES), F32),
            pltpu.SemaphoreType.DMA((6,)),
        ],
        compiler_params=params(),
        cost_estimate=cost(1 << 20, 3 << 20),
        name="unpack",
    )(x, q, k)


def shift(x, k):
    return lax.ppermute(x, "ch", [(i, i ^ k) for i in range(PLANES)])


def exchange(x):
    return lax.all_to_all(x, "ctx", split_axis=0, concat_axis=0, tiled=True)


def local(q, k, v, g, c, filters, genome_blocks):
    forward, inverse = [jnp.asarray(t) for t in dft_tables()]
    plane = lax.axis_index("ch").astype(jnp.int32).reshape(1)
    here = lax.axis_index("ctx").astype(jnp.int32).reshape(1)
    sent = pack(plane, here, q, k, v, g, filters)
    got = exchange(sent.reshape(NCTX, IN_ROWS // 4, 4, LANES))
    own_quarter = got[:MOST, 8].reshape(4 * MOST, LANES)
    near = shift(own_quarter, 3)
    slots, carried, grad_value = lag_part(
        genome_blocks, plane, got.reshape(NCTX * IN_ROWS, LANES), (forward, inverse), g, c
    )
    slots, near = lax.optimization_barrier((slots, near))
    both = shift(jnp.concatenate([own_quarter, near], axis=0), 1)
    lags = [slots[0]] + [shift(slots[i], i) for i in range(1, PLANES)]
    back = back_part(genome_blocks, plane, carried, own_quarter, near, both, forward)
    out = finish(back, lags, inverse).reshape(NCTX, OUT_ROWS // 4, 4, LANES)
    returned = exchange(out).reshape(NCTX * OUT_ROWS, LANES)
    scale = (NCTX * BLOCK) ** (-0.5)
    grad_query, grad_key, grad_filters = unpack(returned, q, k, scale)
    return grad_query, grad_key, grad_value, grad_filters


def solution(mesh):
    split = P("ctx", "ch")
    return jax.shard_map(
        local,
        mesh=mesh,
        in_specs=(split,) * 5 + (P("ctx", None), P()),
        out_specs=(split,) * 4,
        check_vma=False,
    )
```
